32 devices in a mesh: freq: 4 (over x, core), facet: 8 (over z, y).
Axes of the slice: x: 2, y: 2, z: 4, core: 2. Of those that a mesh axis runs over, the one named last changes fastest.
Arguments:
- visibilities: float32 [16, 2, 2048], P('facet', None, 'freq'), may hold values from -6 to 6
- weights: float32 [16, 2048], P('facet', 'freq'), may hold values from 0.1 to 1
- uv_cells: int32 [16, 2, 2048], P('facet', None, 'freq'), may hold values from -16384 to 16383
- flags: int32 [16, 2048], P('facet', 'freq'), may hold values from 0 to 1, as said below
- plan: int32 [16], replicated, may hold values from 0 to 15, each once
- beam: float32 [8, 16], P('facet'), may hold values from 0.2 to 1
- facets: int32 [8, 2], P('facet'), may hold values from 0 to 255
Outputs:
- dirty_image: float32 [8, 128, 128], P('facet', 'freq')
The draws below stay inside these ranges and needn't reach their ends.
Inputs may be any that keep to these rules, and one draw needn't show every extreme that they name: `flags`: in each block, each frequency group's 512 rows hold at most 256 unflagged rows; in every draw some block holds exactly 256 in every group. `plan`: each of the 16 blocks is read at exactly one step.
All inputs are finite; a program needn't handle non-finite values.
Results may differ from the reference program's by a relative error of at most 0.0037.
Values sent between devices are 32-bit elements; how exact they have to be, the bound alone decides.
A program may use at most 64 MiB of HBM per device.

```python
import math
import jax
import jax.numpy as jnp
from jax import lax

P_SIZE = 128
IMG = 32768
KROWS = 512
KEEP = 256
NBLK = 16
KTOT = 2048
N_FACET = 8


def draw_flags(key, part):
    first_key, second_key, third_key = jax.random.split(key, 3)
    groups = KTOT // KROWS
    dropped = jax.random.randint(first_key, (NBLK, groups), 0, KEEP // 2 + 1)
    chosen = jax.random.randint(second_key, (), 0, NBLK)
    dropped = jnp.where(jnp.arange(NBLK)[:, None] == chosen, 0, dropped)
    counts_live = KEEP - dropped
    key_list = jax.random.split(third_key, NBLK * groups)
    ranking = jax.vmap(lambda single: jax.random.permutation(single, KROWS))(key_list)
    ranking = ranking.reshape(NBLK, groups, KROWS)
    return (ranking < counts_live[:, :, None]).astype(jnp.int32).reshape(NBLK, KTOT)


def plant(values, rng, low, high):
    spot = [jax.random.randint(jax.random.fold_in(rng, axis), (), 0, length) for axis, length in enumerate(values.shape)]
    widest = values.shape.index(max(values.shape))
    neighbour = spot[:widest] + [(spot[widest] + 1) % values.shape[widest]] + spot[widest + 1:]
    return values.at[tuple(spot)].set(low).at[tuple(neighbour)].set(high)


def steps_of(own_key, extent, cuts, least, largest):
    def one(axis_at, shards_of):
        steps = jax.random.uniform(jax.random.fold_in(jax.random.fold_in(own_key, 6), axis_at), (shards_of,), jnp.float32, least / len(cuts), largest / len(cuts))
        return jnp.repeat(jnp.exp(steps), extent[axis_at] // shards_of).reshape((-1,) + (1,) * (len(extent) - axis_at - 1))

    factor_of = one(*cuts[0])
    for cut in cuts[1:]:
        factor_of = factor_of * one(*cut)
    return factor_of


def centred(key, dims, spread, most, cuts=(), held_as=jnp.bfloat16):
    factor_of = steps_of(key, dims, cuts, -0.22, 0.18) if cuts else 1.0
    entries = jax.random.normal(key, dims, jnp.float32) * spread * factor_of
    return jnp.minimum(jnp.maximum(entries, -most), most).astype(held_as)


def setup_inputs(seed: int = 0) -> dict:
    keys = jax.random.split(jax.random.key(seed), 8)
    visibilities = centred(keys[0], (NBLK, 2, KTOT), 1.0, 6.0, ((0, 8), (2, 4)), jnp.float32)
    weights = jnp.clip(jnp.exp(math.log(1.0) - 2.3025851 * jax.random.uniform(keys[1], (NBLK, KTOT), jnp.float32) ** steps_of(keys[1], (NBLK, KTOT), ((0, 8), (1, 4)), -0.2, 0.2)), 0.1, 1.0)
    uv_cells = plant(jax.random.randint(keys[2], (NBLK, 2, KTOT), 0 - IMG // 2, IMG // 2), jax.random.fold_in(keys[2], 1), 0 - IMG // 2, (IMG // 2) - 1).astype(jnp.int32)
    flags = draw_flags(jax.random.fold_in(keys[7], 71), 0)
    plan = jax.random.permutation(keys[4], NBLK).astype(jnp.int32)
    beam = jnp.clip(jnp.exp(math.log(1.0) - 1.609438 * jax.random.uniform(keys[5], (N_FACET, NBLK), jnp.float32) ** steps_of(keys[5], (N_FACET, NBLK), ((0, 8),), -0.2, 0.2)), 0.2, 1.0)
    facets = plant(jax.random.randint(keys[6], (N_FACET, 2), 0, IMG // P_SIZE), jax.random.fold_in(keys[6], 1), 0, (IMG // P_SIZE) - 1).astype(jnp.int32)
    return {"visibilities": visibilities, "weights": weights, "uv_cells": uv_cells, "flags": flags, "plan": plan, "beam": beam, "facets": facets}


full_turn = 2.0 * math.pi

def facet_image(samples, facet_col, facet_row):
    pixels = jnp.arange(P_SIZE, dtype=jnp.int32)
    along_l = (facet_col * P_SIZE + pixels - IMG // 2).astype(jnp.int32)
    along_m = (facet_row * P_SIZE + pixels - IMG // 2).astype(jnp.int32)
    u_cells = samples[3].astype(jnp.int32)
    v_cells = samples[4].astype(jnp.int32)
    turn_u = jnp.mod(along_l[:, None] * u_cells[None, :], IMG).astype(jnp.float32) * (full_turn / IMG)
    cos_u = jnp.cos(turn_u)
    sin_u = jnp.sin(turn_u)
    real_part = samples[0] * samples[2]
    imag_part = samples[1] * samples[2]
    left = jnp.concatenate([real_part * cos_u - imag_part * sin_u, -(real_part * sin_u + imag_part * cos_u)], axis=1).astype(jnp.bfloat16)
    turn_v = jnp.mod(v_cells[:, None] * along_m[None, :], IMG).astype(jnp.float32) * (full_turn / IMG)
    right = jnp.concatenate([jnp.cos(turn_v), jnp.sin(turn_v)], axis=0).astype(jnp.bfloat16)
    return jnp.dot(left, right, preferred_element_type=jnp.float32)

def reference(visibilities, weights, uv_cells, flags, plan, beam, facets):
    inverse = jnp.argsort(plan).astype(jnp.int32)
    gains = beam[:, inverse]
    live = weights * flags.astype(jnp.float32)
    uv_float = uv_cells.astype(jnp.float32)

    def one_facet(record):
        position, gain_row = record

        def advance(running, entry):
            vis_block, live_block, uv_block, factor = entry
            samples = jnp.concatenate([vis_block, (live_block * factor)[None, :], uv_block], axis=0)
            return (running + facet_image(samples, position[0], position[1]), None)
        summed, _ = lax.scan(advance, jnp.zeros((P_SIZE, P_SIZE), jnp.float32), (visibilities, live, uv_float, gain_row))
        return summed
    images = lax.map(one_facet, (facets, gains))
    return images * (2.0 / math.sqrt(NBLK * KTOT))
```

```python
import functools
import math

import jax
import jax.numpy as jnp
from jax import lax
from jax.experimental import pallas as pl
from jax.experimental.pallas import tpu as pltpu
from jax.sharding import PartitionSpec as P

P_SIZE = 128
IMG = 32768
KEEP = 256
LANES = 128
HALF = P_SIZE // 2
MESH = pl.DeviceIdType.MESH
NT = (((1,), (1,)), ((), ()))


def cos_sin(x):
    q = x * x
    s = jnp.full_like(q, -1.0 / math.factorial(11))
    for order in (9, 7, 5, 3, 1):
        s = s * q + (-1.0) ** (order // 2) / math.factorial(order)
    c = jnp.full_like(q, 1.0 / math.factorial(12))
    for order in (10, 8, 6, 4, 2, 0):
        c = c * q + (-1.0) ** (order // 2) / math.factorial(order)
    return c, s * x


def times(a, b):
    return a[0] * b[0] - a[1] * b[1], a[0] * b[1] + a[1] * b[0]


def square(a):
    return a[0] * a[0] - a[1] * a[1], 2.0 * (a[0] * a[1])


def powers(z, count):
    found = [None, z]
    for k in range(2, count):
        half = found[k // 2]
        found.append(square(half) if k % 2 == 0 else times(found[k // 2 + 1], half))
    return found


def kept_rows(flags):
    blocks, rows = flags.shape
    pieces = [flags[:, j * LANES:(j + 1) * LANES] for j in range(rows // LANES)]
    stacked = jnp.concatenate(pieces, axis=0)
    lower = lax.broadcasted_iota(jnp.int32, (LANES, LANES), 1) <= lax.broadcasted_iota(
        jnp.int32, (LANES, LANES), 0
    )
    inside = lax.dot_general(
        stacked.astype(jnp.bfloat16),
        jnp.where(lower, 1.0, 0.0).astype(jnp.bfloat16),
        NT,
        preferred_element_type=jnp.float32,
    )
    totals = jnp.sum(stacked, axis=1, keepdims=True)
    before = jnp.zeros((blocks, 1), jnp.float32)
    places = []
    for j, piece in enumerate(pieces):
        own = slice(j * blocks, (j + 1) * blocks)
        places.append(jnp.where(piece > 0.5, inside[own] + before - 1.0, -1.0))
        before = before + totals[own]
    return jnp.concatenate(places, axis=1)


def split3(x):
    high = x.astype(jnp.bfloat16).astype(jnp.float32)
    rest = x - high
    middle = rest.astype(jnp.bfloat16).astype(jnp.float32)
    low = rest - middle
    return jnp.concatenate([high, middle, low, jnp.zeros_like(x)], axis=0).astype(jnp.bfloat16)


def kernel(
    n, nf, scale,
    vis_hbm, w_hbm, uv_hbm, flags_hbm, plan_hbm, beam_hbm, facets_hbm,
    out_ref,
    vis, wts, uv, flg, plan, beam, facets,
    buf, fine_c, fine_s, outer_c, outer_s, half_c, half_s, amp, stage, rbuf,
    in_sem, send_sem, recv_sem, rsend_sem, rrecv_sem,
):
    mf = lax.axis_index("freq")
    me = lax.axis_index("facet")
    barrier = pltpu.get_barrier_semaphore()
    loads = [
        pltpu.make_async_copy(src, dst, in_sem.at[k])
        for k, (src, dst) in enumerate(
            [(flags_hbm, flg), (vis_hbm, vis), (w_hbm, wts), (uv_hbm, uv),
             (plan_hbm, plan), (beam_hbm, beam), (facets_hbm, facets)]
        )
    ]
    for load in loads:
        load.start()
    for j in range(1, n):
        pl.semaphore_signal(
            barrier, inc=1, device_id={"facet": lax.rem(me + j, n)}, device_id_type=MESH
        )
    for j in range(1, nf):
        pl.semaphore_signal(
            barrier, inc=1, device_id={"freq": lax.rem(mf + j, nf)}, device_id_type=MESH
        )
    for load in loads:
        load.wait()

    flags = flg[...].astype(jnp.float32)
    place = kept_rows(flags).astype(jnp.int32)
    live = wts[...] * flags
    blocks, rows = flags.shape
    per_block = KEEP // LANES
    four = blocks * per_block
    slot_at = lax.broadcasted_iota(jnp.int32, (KEEP, rows), 0)
    for b in range(blocks):
        chosen = jnp.where(place[b:b + 1, :] == slot_at, 1.0, 0.0).astype(jnp.bfloat16)
        values = jnp.concatenate([vis[b] * live[b:b + 1, :], uv[b].astype(jnp.float32)], axis=0)
        packed = lax.dot_general(split3(values), chosen, NT, preferred_element_type=jnp.float32)
        packed = packed[0:4] + packed[4:8] + packed[8:12]
        for q in range(4):
            for h in range(per_block):
                row = (q % 2) * four + b * per_block + h
                buf[0, q // 2, row:row + 1, :] = packed[q:q + 1, h * LANES:(h + 1) * LANES]

    pl.semaphore_wait(barrier, n - 1 + nf - 1)
    sends = []
    for j in range(1, n):
        sends.append(
            pltpu.make_async_remote_copy(
                src_ref=buf.at[0],
                dst_ref=buf.at[j],
                send_sem=send_sem.at[j],
                recv_sem=recv_sem.at[j],
                device_id={"facet": lax.rem(me + j, n)},
                device_id_type=MESH,
            )
        )
        sends[-1].start()

    tall = 2 * four
    steps = plan.shape[1]
    row_at = lax.broadcasted_iota(jnp.int32, (n * tall, steps), 0)
    source = me - row_at // tall
    source = jnp.where(source < 0, source + n, source)
    block = source * blocks + (row_at % four) // per_block
    gains = jnp.sum(jnp.where(block == plan[...], beam[...] * scale, 0.0), axis=1, keepdims=True)

    high_row = lax.broadcasted_iota(jnp.int32, (tall, LANES), 0) < four
    first = facets[...] * P_SIZE - IMG // 2
    factor = jnp.where(high_row, 2 * first[:, 0:1] + (P_SIZE - 1), 2 * first[:, 1:2])
    sign = jnp.where(high_row, -1.0, 1.0)

    def swap(x):
        return jnp.concatenate([x[:, four:], x[:, :four]], axis=1)

    def tabulate(lo, hi):
        count = hi - lo
        cells = buf[lo:hi, 1]
        half = cos_sin(cells * (math.pi / IMG))
        turns = cells.astype(jnp.int32) * factor[None]
        turns = turns + swap(turns)
        turns = ((turns + IMG) & (2 * IMG - 1)) - IMG
        base = square(cos_sin(turns.astype(jnp.float32) * (math.pi / (2 * IMG))))
        x = buf[lo:hi, 0] * gains[lo * tall:hi * tall].reshape(count, tall, 1)
        amp[lo:hi] = x * base[0] + swap(x) * (base[1] * sign[None])
        half_c[lo:hi] = half[0]
        half_s[lo:hi] = half[1]
        z = square(half)
        one = (jnp.ones_like(z[0]), jnp.zeros_like(z[0]))
        fine = powers(z, 8)
        fine[0] = one
        outer = powers(square(fine[4]), P_SIZE // 8)
        outer[0] = one
        for refs, table in (((fine_c, fine_s), fine), ((outer_c, outer_s), outer)):
            for part in range(2):
                for k, entry in enumerate(table):
                    for i in range(count):
                        at = ((lo + i) * len(table) + k) * tall
                        refs[part][at:at + tall, :] = entry[part][i]

    def image_terms(slot, sums):
        cu, su, re, im = [], [], [], []
        for r in range(four):
            def pick(refs, table_rows, row):
                at = pl.ds(slot * (8 * tall) + row, 8, stride=tall)
                return refs[0][at, :], refs[1][at, :]

            def line(refs, row):
                return refs[0][slot, row:row + 1, :], refs[1][slot, row:row + 1, :]

            def outer_line(k, row):
                at = pl.ds(slot * (16 * tall) + k * tall + row, 1)
                return outer_c[at, :], outer_s[at, :]

            u = times(line((half_c, half_s), r), pick((fine_c, fine_s), 8, r))
            v = times(
                (amp[slot, r:r + 1, :], amp[slot, four + r:four + r + 1, :]),
                pick((fine_c, fine_s), 8, four + r),
            )
            left = [u] + [times(outer_line(k, r), u) for k in range(1, HALF // 8)]
            right = [v] + [times(outer_line(k, four + r), v) for k in range(1, P_SIZE // 8)]
            for kept, table, part in ((cu, left, 0), (su, left, 1), (re, right, 0), (im, right, 1)):
                kept.append(
                    jnp.concatenate([entry[part] for entry in table], axis=0).astype(jnp.bfloat16)
                )
        cu, su, re, im = (jnp.concatenate(kept, axis=1) for kept in (cu, su, re, im))
        return (
            sums[0] + lax.dot_general(cu, re, NT, preferred_element_type=jnp.float32),
            sums[1] + lax.dot_general(su, im, NT, preferred_element_type=jnp.float32),
        )

    zero = jnp.zeros((HALF, P_SIZE), jnp.float32)
    tabulate(0, 1)
    sums = image_terms(0, (zero, zero))
    for j in range(1, n):
        sends[j - 1].wait_recv()
    tabulate(1, n)
    even, odd = lax.fori_loop(1, n, image_terms, sums)

    share = P_SIZE // nf
    for f in range(nf):
        if f < nf // 2:
            at = (nf // 2 - 1 - f) * share
            stage[f] = even[at:at + share] + odd[at:at + share]
        else:
            at = (f - nf // 2) * share
            stage[f] = even[at:at + share] - odd[at:at + share]
    exchanges = []
    for j in range(1, nf):
        to = lax.rem(mf + j, nf)
        exchanges.append(
            pltpu.make_async_remote_copy(
                src_ref=stage.at[to],
                dst_ref=rbuf.at[j],
                send_sem=rsend_sem.at[j],
                recv_sem=rrecv_sem.at[j],
                device_id={"freq": to},
                device_id_type=MESH,
            )
        )
        exchanges[-1].start()
    total = stage[mf]
    for j in range(1, nf):
        exchanges[j - 1].wait_recv()
        total = total + rbuf[j]

    row8 = lax.broadcasted_iota(jnp.int32, (8, P_SIZE), 0)
    mirrored = []
    for k in reversed(range(share // 8)):
        y = pltpu.roll(total[k * 8:(k + 1) * 8], 4, 0)
        y = jnp.where((row8 & 2) != 0, pltpu.roll(y, 2, 0), pltpu.roll(y, 6, 0))
        y = jnp.where((row8 & 1) != 0, pltpu.roll(y, 1, 0), pltpu.roll(y, 7, 0))
        mirrored.append(y)
    mirrored = jnp.concatenate(mirrored, axis=0)
    out_ref[0] = jnp.where(mf < nf // 2, mirrored, total)
    for copy in sends + exchanges:
        copy.wait_send()


def body(n, nf, scale, visibilities, weights, uv_cells, flags, plan, beam, facets):
    blocks, _, rows = visibilities.shape
    four = blocks * (KEEP // LANES)
    tall = 2 * four
    share = P_SIZE // nf
    steps = plan.shape[0]
    f32, i32 = jnp.float32, jnp.int32
    return pl.pallas_call(
        functools.partial(kernel, n, nf, scale),
        out_shape=jax.ShapeDtypeStruct((1, share, P_SIZE), f32),
        in_specs=[pl.BlockSpec(memory_space=pl.ANY)] * 7,
        out_specs=pl.BlockSpec(memory_space=pltpu.VMEM),
        scratch_shapes=[
            pltpu.VMEM((blocks, 2, rows), f32),
            pltpu.VMEM((blocks, rows), f32),
            pltpu.VMEM((blocks, 2, rows), i32),
            pltpu.VMEM((blocks, rows), i32),
            pltpu.VMEM((1, steps), i32),
            pltpu.VMEM((1, steps), f32),
            pltpu.VMEM((1, 2), i32),
            pltpu.VMEM((n, 2, tall, LANES), f32),
            pltpu.VMEM((n * 8 * tall, LANES), f32),
            pltpu.VMEM((n * 8 * tall, LANES), f32),
            pltpu.VMEM((n * 16 * tall, LANES), f32),
            pltpu.VMEM((n * 16 * tall, LANES), f32),
            pltpu.VMEM((n, tall, LANES), f32),
            pltpu.VMEM((n, tall, LANES), f32),
            pltpu.VMEM((n, tall, LANES), f32),
            pltpu.VMEM((nf, share, P_SIZE), f32),
            pltpu.VMEM((nf, share, P_SIZE), f32),
            pltpu.SemaphoreType.DMA((7,)),
            pltpu.SemaphoreType.DMA((n,)),
            pltpu.SemaphoreType.DMA((n,)),
            pltpu.SemaphoreType.DMA((nf,)),
            pltpu.SemaphoreType.DMA((nf,)),
        ],
        compiler_params=pltpu.CompilerParams(
            collective_id=0, has_side_effects=True, vmem_limit_bytes=32 * 1024 * 1024
        ),
        name="facet_image",
    )(visibilities, weights, uv_cells, flags, plan.reshape(1, steps), beam, facets)


def solution(mesh):
    n, nf = mesh.shape["facet"], mesh.shape["freq"]
    in_specs = (
        P("facet", None, "freq"),
        P("facet", "freq"),
        P("facet", None, "freq"),
        P("facet", "freq"),
        P(),
        P("facet", None),
        P("facet", None),
    )
    out_specs = P("facet", "freq", None)

    def whole(visibilities, *others):
        scale = 2.0 / math.sqrt(visibilities.shape[0] * visibilities.shape[2])
        return jax.shard_map(
            functools.partial(body, n, nf, scale),
            mesh=mesh, in_specs=in_specs, out_specs=out_specs, check_vma=False,
        )(visibilities, *others)

    return whole
```

```python
import functools
import math

import jax
import jax.numpy as jnp
from jax import lax
from jax.experimental import pallas as pl
from jax.experimental.pallas import tpu as pltpu
from jax.sharding import PartitionSpec as P

P_SIZE = 128
IMG = 32768
KEEP = 256
LANES = 128
HALF = P_SIZE // 2
MESH = pl.DeviceIdType.MESH
NT = (((1,), (1,)), ((), ()))


def cos_sin(x):
    q = x * x
    s = jnp.full_like(q, -1.0 / math.factorial(11))
    for order in (9, 7, 5, 3, 1):
        s = s * q + (-1.0) ** (order // 2) / math.factorial(order)
    c = jnp.full_like(q, 1.0 / math.factorial(12))
    for order in (10, 8, 6, 4, 2, 0):
        c = c * q + (-1.0) ** (order // 2) / math.factorial(order)
    return c, s * x


def times(a, b):
    return a[0] * b[0] - a[1] * b[1], a[0] * b[1] + a[1] * b[0]


def square(a):
    return a[0] * a[0] - a[1] * a[1], 2.0 * (a[0] * a[1])


def powers(z, count):
    found = [None, z]
    for k in range(2, count):
        half = found[k // 2]
        found.append(square(half) if k % 2 == 0 else times(found[k // 2 + 1], half))
    return found


def kept_rows(flags):
    blocks, rows = flags.shape
    pieces = [flags[:, j * LANES:(j + 1) * LANES] for j in range(rows // LANES)]
    stacked = jnp.concatenate(pieces, axis=0)
    lower = lax.broadcasted_iota(jnp.int32, (LANES, LANES), 1) <= lax.broadcasted_iota(
        jnp.int32, (LANES, LANES), 0
    )
    inside = lax.dot_general(
        stacked.astype(jnp.bfloat16),
        jnp.where(lower, 1.0, 0.0).astype(jnp.bfloat16),
        NT,
        preferred_element_type=jnp.float32,
    )
    totals = jnp.sum(stacked, axis=1, keepdims=True)
    before = jnp.zeros((blocks, 1), jnp.float32)
    places = []
    for j, piece in enumerate(pieces):
        own = slice(j * blocks, (j + 1) * blocks)
        places.append(jnp.where(piece > 0.5, inside[own] + before - 1.0, -1.0))
        before = before + totals[own]
    return jnp.concatenate(places, axis=1)


def split3(x):
    high = x.astype(jnp.bfloat16).astype(jnp.float32)
    rest = x - high
    middle = rest.astype(jnp.bfloat16).astype(jnp.float32)
    low = rest - middle
    return jnp.concatenate([high, middle, low, jnp.zeros_like(x)], axis=0).astype(jnp.bfloat16)


def kernel(
    n, nf, scale,
    vis_hbm, w_hbm, uv_hbm, flags_hbm, plan_hbm, beam_hbm, facets_hbm,
    out_ref,
    vis, wts, uv, flg, plan, beam, facets,
    buf, fine_c, fine_s, outer_c, outer_s, half_c, half_s, amp, stage, rbuf,
    in_sem, send_sem, recv_sem, rsend_sem, rrecv_sem,
):
    mf = lax.axis_index("freq")
    me = lax.axis_index("facet")
    barrier = pltpu.get_barrier_semaphore()
    loads = [
        pltpu.make_async_copy(src, dst, in_sem.at[k])
        for k, (src, dst) in enumerate(
            [(flags_hbm, flg), (vis_hbm, vis), (w_hbm, wts), (uv_hbm, uv),
             (plan_hbm, plan), (beam_hbm, beam), (facets_hbm, facets)]
        )
    ]
    for load in loads:
        load.start()
    for j in range(1, n):
        pl.semaphore_signal(
            barrier, inc=1, device_id={"facet": lax.rem(me + j, n)}, device_id_type=MESH
        )
    for j in range(1, nf):
        pl.semaphore_signal(
            barrier, inc=1, device_id={"freq": lax.rem(mf + j, nf)}, device_id_type=MESH
        )
    for load in loads:
        load.wait()

    flags = flg[...].astype(jnp.float32)
    place = kept_rows(flags).astype(jnp.int32)
    live = wts[...] * flags
    blocks, rows = flags.shape
    per_block = KEEP // LANES
    four = blocks * per_block
    slot_at = lax.broadcasted_iota(jnp.int32, (KEEP, rows), 0)
    for b in range(blocks):
        chosen = jnp.where(place[b:b + 1, :] == slot_at, 1.0, 0.0).astype(jnp.bfloat16)
        values = jnp.concatenate([vis[b] * live[b:b + 1, :], uv[b].astype(jnp.float32)], axis=0)
        packed = lax.dot_general(split3(values), chosen, NT, preferred_element_type=jnp.float32)
        packed = packed[0:4] + packed[4:8] + packed[8:12]
        for q in range(4):
            for h in range(per_block):
                row = (q % 2) * four + b * per_block + h
                buf[0, q // 2, row:row + 1, :] = packed[q:q + 1, h * LANES:(h + 1) * LANES]

    pl.semaphore_wait(barrier, n - 1 + nf - 1)
    sends = []
    for j in range(1, n):
        sends.append(
            pltpu.make_async_remote_copy(
                src_ref=buf.at[0],
                dst_ref=buf.at[j],
                send_sem=send_sem.at[j],
                recv_sem=recv_sem.at[j],
                device_id={"facet": lax.rem(me + j, n)},
                device_id_type=MESH,
            )
        )
        sends[-1].start()

    tall = 2 * four
    steps = plan.shape[1]
    row_at = lax.broadcasted_iota(jnp.int32, (n * tall, steps), 0)
    source = me - row_at // tall
    source = jnp.where(source < 0, source + n, source)
    block = source * blocks + (row_at % four) // per_block
    gains = jnp.sum(jnp.where(block == plan[...], beam[...] * scale, 0.0), axis=1, keepdims=True)

    high_row = lax.broadcasted_iota(jnp.int32, (tall, LANES), 0) < four
    first = facets[...] * P_SIZE - IMG // 2
    factor = jnp.where(high_row, 2 * first[:, 0:1] + (P_SIZE - 1), 2 * first[:, 1:2])
    sign = jnp.where(high_row, -1.0, 1.0)

    def swap(x):
        return jnp.concatenate([x[:, four:], x[:, :four]], axis=1)

    def tabulate(lo, hi):
        count = hi - lo
        cells = buf[lo:hi, 1]
        half = cos_sin(cells * (math.pi / IMG))
        turns = cells.astype(jnp.int32) * factor[None]
        turns = turns + swap(turns)
        turns = ((turns + IMG) & (2 * IMG - 1)) - IMG
        base = square(cos_sin(turns.astype(jnp.float32) * (math.pi / (2 * IMG))))
        x = buf[lo:hi, 0] * gains[lo * tall:hi * tall].reshape(count, tall, 1)
        amp[lo:hi] = x * base[0] + swap(x) * (base[1] * sign[None])
        half_c[lo:hi] = half[0]
        half_s[lo:hi] = half[1]
        z = square(half)
        one = (jnp.ones_like(z[0]), jnp.zeros_like(z[0]))
        fine = powers(z, 8)
        fine[0] = one
        outer = powers(square(fine[4]), P_SIZE // 8)
        outer[0] = one
        for refs, table in (((fine_c, fine_s), fine), ((outer_c, outer_s), outer)):
            for part in range(2):
                for k, entry in enumerate(table):
                    for i in range(count):
                        at = ((lo + i) * len(table) + k) * tall
                        refs[part][at:at + tall, :] = entry[part][i]

    def image_terms(slot, sums):
        cu, su, re, im = [], [], [], []
        for r in range(four):
            def pick(refs, table_rows, row):
                at = pl.ds(slot * (8 * tall) + row, 8, stride=tall)
                return refs[0][at, :], refs[1][at, :]

            def line(refs, row):
                return refs[0][slot, row:row + 1, :], refs[1][slot, row:row + 1, :]

            def outer_line(k, row):
                at = pl.ds(slot * (16 * tall) + k * tall + row, 1)
                return outer_c[at, :], outer_s[at, :]

            u = times(line((half_c, half_s), r), pick((fine_c, fine_s), 8, r))
            v = times(
                (amp[slot, r:r + 1, :], amp[slot, four + r:four + r + 1, :]),
                pick((fine_c, fine_s), 8, four + r),
            )
            left = [u] + [times(outer_line(k, r), u) for k in range(1, HALF // 8)]
            right = [v] + [times(outer_line(k, four + r), v) for k in range(1, P_SIZE // 8)]
            for kept, table, part in ((cu, left, 0), (su, left, 1), (re, right, 0), (im, right, 1)):
                kept.append(
                    jnp.concatenate([entry[part] for entry in table], axis=0).astype(jnp.bfloat16)
                )
        cu, su, re, im = (jnp.concatenate(kept, axis=1) for kept in (cu, su, re, im))
        return (
            sums[0] + lax.dot_general(cu, re, NT, preferred_element_type=jnp.float32),
            sums[1] + lax.dot_general(su, im, NT, preferred_element_type=jnp.float32),
        )

    zero = jnp.zeros((HALF, P_SIZE), jnp.float32)
    tabulate(0, 1)
    sums = image_terms(0, (zero, zero))
    for j in range(1, n):
        sends[j - 1].wait_recv()
    tabulate(1, n)
    even, odd = lax.fori_loop(1, n, image_terms, sums, unroll=n - 1 if n <= 8 else 1)

    share = P_SIZE // nf
    for f in range(nf):
        if f < nf // 2:
            at = (nf // 2 - 1 - f) * share
            stage[f] = even[at:at + share] + odd[at:at + share]
        else:
            at = (f - nf // 2) * share
            stage[f] = even[at:at + share] - odd[at:at + share]
    exchanges = []
    for j in range(1, nf):
        to = lax.rem(mf + j, nf)
        exchanges.append(
            pltpu.make_async_remote_copy(
                src_ref=stage.at[to],
                dst_ref=rbuf.at[j],
                send_sem=rsend_sem.at[j],
                recv_sem=rrecv_sem.at[j],
                device_id={"freq": to},
                device_id_type=MESH,
            )
        )
        exchanges[-1].start()
    total = stage[mf]
    for j in range(1, nf):
        exchanges[j - 1].wait_recv()
        total = total + rbuf[j]

    row8 = lax.broadcasted_iota(jnp.int32, (8, P_SIZE), 0)
    mirrored = []
    for k in reversed(range(share // 8)):
        y = pltpu.roll(total[k * 8:(k + 1) * 8], 4, 0)
        y = jnp.where((row8 & 2) != 0, pltpu.roll(y, 2, 0), pltpu.roll(y, 6, 0))
        y = jnp.where((row8 & 1) != 0, pltpu.roll(y, 1, 0), pltpu.roll(y, 7, 0))
        mirrored.append(y)
    mirrored = jnp.concatenate(mirrored, axis=0)
    out_ref[0] = jnp.where(mf < nf // 2, mirrored, total)
    for copy in sends + exchanges:
        copy.wait_send()


def body(n, nf, scale, visibilities, weights, uv_cells, flags, plan, beam, facets):
    blocks, _, rows = visibilities.shape
    four = blocks * (KEEP // LANES)
    tall = 2 * four
    share = P_SIZE // nf
    steps = plan.shape[0]
    f32, i32 = jnp.float32, jnp.int32
    return pl.pallas_call(
        functools.partial(kernel, n, nf, scale),
        out_shape=jax.ShapeDtypeStruct((1, share, P_SIZE), f32),
        in_specs=[pl.BlockSpec(memory_space=pltpu.HBM)] * 7,
        out_specs=pl.BlockSpec(memory_space=pltpu.VMEM),
        scratch_shapes=[
            pltpu.VMEM((blocks, 2, rows), f32),
            pltpu.VMEM((blocks, rows), f32),
            pltpu.VMEM((blocks, 2, rows), i32),
            pltpu.VMEM((blocks, rows), i32),
            pltpu.VMEM((1, steps), i32),
            pltpu.VMEM((1, steps), f32),
            pltpu.VMEM((1, 2), i32),
            pltpu.VMEM((n, 2, tall, LANES), f32),
            pltpu.VMEM((n * 8 * tall, LANES), f32),
            pltpu.VMEM((n * 8 * tall, LANES), f32),
            pltpu.VMEM((n * 16 * tall, LANES), f32),
            pltpu.VMEM((n * 16 * tall, LANES), f32),
            pltpu.VMEM((n, tall, LANES), f32),
            pltpu.VMEM((n, tall, LANES), f32),
            pltpu.VMEM((n, tall, LANES), f32),
            pltpu.VMEM((nf, share, P_SIZE), f32),
            pltpu.VMEM((nf, share, P_SIZE), f32),
            pltpu.SemaphoreType.DMA((7,)),
            pltpu.SemaphoreType.DMA((n,)),
            pltpu.SemaphoreType.DMA((n,)),
            pltpu.SemaphoreType.DMA((nf,)),
            pltpu.SemaphoreType.DMA((nf,)),
        ],
        compiler_params=pltpu.CompilerParams(
            collective_id=0, has_side_effects=True, vmem_limit_bytes=62 * 1024 * 1024
        ),
        name="facet_image",
    )(visibilities, weights, uv_cells, flags, plan.reshape(1, steps), beam, facets)


def solution(mesh):
    n, nf = mesh.shape["facet"], mesh.shape["freq"]
    in_specs = (
        P("facet", None, "freq"),
        P("facet", "freq"),
        P("facet", None, "freq"),
        P("facet", "freq"),
        P(),
        P("facet", None),
        P("facet", None),
    )
    out_specs = P("facet", "freq", None)

    def whole(visibilities, *others):
        scale = 2.0 / math.sqrt(visibilities.shape[0] * visibilities.shape[2])
        return jax.shard_map(
            functools.partial(body, n, nf, scale),
            mesh=mesh, in_specs=in_specs, out_specs=out_specs, check_vma=False,
        )(visibilities, *others)

    return whole
```

```python
import functools
import math

import jax
import jax.numpy as jnp
from jax import lax
from jax.experimental import pallas as pl
from jax.experimental.pallas import tpu as pltpu
from jax.sharding import PartitionSpec as P

P_SIZE = 128
IMG = 32768
KEEP = 256
LANES = 128
HALF = P_SIZE // 2
FINE = 16
COARSE = P_SIZE // FINE
MESH = pl.DeviceIdType.MESH
NT = (((1,), (1,)), ((), ()))


def cos_sin(x):
    q = x * x
    s = jnp.full_like(q, -1.0 / math.factorial(11))
    for order in (9, 7, 5, 3, 1):
        s = s * q + (-1.0) ** (order // 2) / math.factorial(order)
    c = jnp.full_like(q, 1.0 / math.factorial(12))
    for order in (10, 8, 6, 4, 2, 0):
        c = c * q + (-1.0) ** (order // 2) / math.factorial(order)
    return c, s * x


def times(a, b):
    return a[0] * b[0] - a[1] * b[1], a[0] * b[1] + a[1] * b[0]


def square(a):
    return a[0] * a[0] - a[1] * a[1], 2.0 * (a[0] * a[1])


def powers(z, count):
    found = [None, z]
    for k in range(2, count):
        half = found[k // 2]
        found.append(square(half) if k % 2 == 0 else times(found[k // 2 + 1], half))
    return found


def partner(me, j, n):
    assert n & (n - 1) == 0
    found, bit = 0, 1
    while bit < n:
        own = lax.rem(me // bit, 2)
        found = found + bit * (1 - own if j & bit else own)
        bit *= 2
    return found


def arrival_groups(n):
    return [(0, 1)] + [(lo, hi) for lo, hi in ((1, n // 2), (n // 2, n)) if lo < hi]


def kept_rows(flags):
    blocks, rows = flags.shape
    pieces = [flags[:, j * LANES:(j + 1) * LANES] for j in range(rows // LANES)]
    stacked = jnp.concatenate(pieces, axis=0)
    lower = lax.broadcasted_iota(jnp.int32, (LANES, LANES), 1) <= lax.broadcasted_iota(
        jnp.int32, (LANES, LANES), 0
    )
    inside = lax.dot_general(
        stacked.astype(jnp.bfloat16),
        jnp.where(lower, 1.0, 0.0).astype(jnp.bfloat16),
        NT,
        preferred_element_type=jnp.float32,
    )
    totals = jnp.sum(stacked, axis=1, keepdims=True)
    before = jnp.zeros((blocks, 1), jnp.float32)
    places = []
    for j, piece in enumerate(pieces):
        own = slice(j * blocks, (j + 1) * blocks)
        places.append(jnp.where(piece > 0.5, inside[own] + before - 1.0, -1.0))
        before = before + totals[own]
    return jnp.concatenate(places, axis=1)


def split3(x):
    high = x.astype(jnp.bfloat16).astype(jnp.float32)
    rest = x - high
    middle = rest.astype(jnp.bfloat16).astype(jnp.float32)
    low = rest - middle
    return jnp.concatenate([high, middle, low, jnp.zeros_like(x)], axis=0).astype(jnp.bfloat16)


def kernel(
    n, nf, scale,
    vis_hbm, w_hbm, uv_hbm, flags_hbm, plan_hbm, beam_hbm, facets_hbm,
    out_ref,
    vis, wts, uv, flg, plan, beam, facets,
    buf, fine_c, fine_s, outer_c, outer_s, half_c, half_s, amp, stage, rbuf,
    in_sem, send_sem, recv_sem, rsend_sem, rrecv_sem,
):
    mf = lax.axis_index("freq")
    me = lax.axis_index("facet")
    barrier = pltpu.get_barrier_semaphore()
    loads = [
        pltpu.make_async_copy(src, dst, in_sem.at[k])
        for k, (src, dst) in enumerate(
            [(flags_hbm, flg), (vis_hbm, vis), (w_hbm, wts), (uv_hbm, uv),
             (plan_hbm, plan), (beam_hbm, beam), (facets_hbm, facets)]
        )
    ]
    for load in loads:
        load.start()
    peers = [partner(me, j, n) for j in range(n)]
    for j in reversed(range(1, n)):
        pl.semaphore_signal(barrier, inc=1, device_id={"facet": peers[j]}, device_id_type=MESH)
    for j in range(1, nf):
        pl.semaphore_signal(
            barrier, inc=1, device_id={"freq": lax.rem(mf + j, nf)}, device_id_type=MESH
        )
    for load in loads:
        load.wait()

    flags = flg[...].astype(jnp.float32)
    place = kept_rows(flags).astype(jnp.int32)
    live = wts[...] * flags
    blocks, rows = flags.shape
    per_block = KEEP // LANES
    four = blocks * per_block
    slot_at = lax.broadcasted_iota(jnp.int32, (KEEP, rows), 0)
    for b in range(blocks):
        chosen = jnp.where(place[b:b + 1, :] == slot_at, 1.0, 0.0).astype(jnp.bfloat16)
        values = jnp.concatenate([vis[b] * live[b:b + 1, :], uv[b].astype(jnp.float32)], axis=0)
        packed = lax.dot_general(split3(values), chosen, NT, preferred_element_type=jnp.float32)
        packed = packed[0:4] + packed[4:8] + packed[8:12]
        for q in range(4):
            for h in range(per_block):
                row = (q % 2) * four + b * per_block + h
                buf[0, q // 2, row:row + 1, :] = packed[q:q + 1, h * LANES:(h + 1) * LANES]

    pl.semaphore_wait(barrier, n - 1 + nf - 1)
    sends = [
        pltpu.make_async_remote_copy(
            src_ref=buf.at[0],
            dst_ref=buf.at[j],
            send_sem=send_sem.at[j],
            recv_sem=recv_sem.at[j],
            device_id={"facet": peers[j]},
            device_id_type=MESH,
        )
        for j in range(1, n)
    ]
    for send in reversed(sends):
        send.start()

    tall = 2 * four
    steps = plan.shape[1]
    row_at = lax.broadcasted_iota(jnp.int32, (tall, steps), 0)
    local = sum(
        jnp.where((row_at >= h * four + b * per_block) & (row_at < h * four + (b + 1) * per_block), b, 0)
        for h in range(2) for b in range(1, blocks)
    )
    read = plan[...] - local
    gain = beam[...] * scale
    gains = [
        jnp.sum(jnp.where(read == peers[j] * blocks, gain, 0.0), axis=1, keepdims=True)
        for j in range(n)
    ]

    high_row = lax.broadcasted_iota(jnp.int32, (tall, LANES), 0) < four
    first = facets[...] * P_SIZE - IMG // 2
    factor = jnp.where(high_row, 2 * first[:, 0:1] + (P_SIZE - 1), 2 * first[:, 1:2])
    sign = jnp.where(high_row, -1.0, 1.0)

    def swap(x):
        return jnp.concatenate([x[:, four:], x[:, :four]], axis=1)

    def tabulate(lo, hi):
        count = hi - lo
        cells = buf[lo:hi, 1]
        half = cos_sin(cells * (math.pi / IMG))
        turns = cells.astype(jnp.int32) * factor[None]
        turns = turns + swap(turns)
        turns = ((turns + IMG) & (2 * IMG - 1)) - IMG
        base = square(cos_sin(turns.astype(jnp.float32) * (math.pi / (2 * IMG))))
        x = buf[lo:hi, 0] * jnp.stack(
            [jnp.broadcast_to(gains[j], (tall, LANES)) for j in range(lo, hi)]
        )
        amp[lo:hi] = x * base[0] + swap(x) * (base[1] * sign[None])
        half_c[lo:hi] = half[0]
        half_s[lo:hi] = half[1]
        z = square(half)
        one = (jnp.ones_like(z[0]), jnp.zeros_like(z[0]))
        fine = powers(z, FINE)
        fine[0] = one
        outer = powers(square(fine[FINE // 2]), COARSE)
        outer[0] = one
        for refs, table in (((fine_c, fine_s), fine), ((outer_c, outer_s), outer)):
            for part in range(2):
                for k, entry in enumerate(table):
                    for i in range(count):
                        at = ((lo + i) * len(table) + k) * tall
                        refs[part][at:at + tall, :] = entry[part][i]

    def image_terms(slot, sums):
        cu, su, re, im = [], [], [], []
        for r in range(four):
            def pick(row):
                at = pl.ds(slot * (FINE * tall) + row, FINE, stride=tall)
                return fine_c[at, :], fine_s[at, :]

            def line(refs, row):
                return refs[0][slot, row:row + 1, :], refs[1][slot, row:row + 1, :]

            def outer_line(k, row):
                at = pl.ds(slot * (COARSE * tall) + k * tall + row, 1)
                return outer_c[at, :], outer_s[at, :]

            u = times(line((half_c, half_s), r), pick(r))
            v = times(
                (amp[slot, r:r + 1, :], amp[slot, four + r:four + r + 1, :]),
                pick(four + r),
            )
            left = [u] + [times(outer_line(k, r), u) for k in range(1, HALF // FINE)]
            right = [v] + [times(outer_line(k, four + r), v) for k in range(1, COARSE)]
            for kept, table, part in ((cu, left, 0), (su, left, 1), (re, right, 0), (im, right, 1)):
                kept.append(
                    jnp.concatenate([entry[part] for entry in table], axis=0).astype(jnp.bfloat16)
                )
        cu, su, re, im = (jnp.concatenate(kept, axis=1) for kept in (cu, su, re, im))
        return (
            sums[0] + lax.dot_general(cu, re, NT, preferred_element_type=jnp.float32),
            sums[1] + lax.dot_general(su, im, NT, preferred_element_type=jnp.float32),
        )

    sums = (jnp.zeros((HALF, P_SIZE), jnp.float32),) * 2
    for lo, hi in arrival_groups(n):
        for j in range(max(lo, 1), hi):
            sends[j - 1].wait_recv()
        tabulate(lo, hi)
        sums = lax.fori_loop(lo, hi, image_terms, sums, unroll=hi - lo if hi - lo <= 4 else 1)
    even, odd = sums

    share = P_SIZE // nf
    for f in range(nf):
        if f < nf // 2:
            at = (nf // 2 - 1 - f) * share
            stage[f] = even[at:at + share] + odd[at:at + share]
        else:
            at = (f - nf // 2) * share
            stage[f] = even[at:at + share] - odd[at:at + share]
    exchanges = []
    for j in range(1, nf):
        to = lax.rem(mf + j, nf)
        exchanges.append(
            pltpu.make_async_remote_copy(
                src_ref=stage.at[to],
                dst_ref=rbuf.at[j],
                send_sem=rsend_sem.at[j],
                recv_sem=rrecv_sem.at[j],
                device_id={"freq": to},
                device_id_type=MESH,
            )
        )
        exchanges[-1].start()
    total = stage[mf]
    for j in range(1, nf):
        exchanges[j - 1].wait_recv()
        total = total + rbuf[j]

    row8 = lax.broadcasted_iota(jnp.int32, (8, P_SIZE), 0)
    mirrored = []
    for k in reversed(range(share // 8)):
        y = pltpu.roll(total[k * 8:(k + 1) * 8], 4, 0)
        y = jnp.where((row8 & 2) != 0, pltpu.roll(y, 2, 0), pltpu.roll(y, 6, 0))
        y = jnp.where((row8 & 1) != 0, pltpu.roll(y, 1, 0), pltpu.roll(y, 7, 0))
        mirrored.append(y)
    mirrored = jnp.concatenate(mirrored, axis=0)
    out_ref[0] = jnp.where(mf < nf // 2, mirrored, total)
    for copy in sends + exchanges:
        copy.wait_send()


def body(n, nf, scale, visibilities, weights, uv_cells, flags, plan, beam, facets):
    blocks, _, rows = visibilities.shape
    four = blocks * (KEEP // LANES)
    tall = 2 * four
    share = P_SIZE // nf
    steps = plan.shape[0]
    f32, i32 = jnp.float32, jnp.int32
    return pl.pallas_call(
        functools.partial(kernel, n, nf, scale),
        out_shape=pltpu.VMEM((1, share, P_SIZE), f32),
        in_specs=[pl.BlockSpec(memory_space=pltpu.HBM)] * 7,
        out_specs=pl.BlockSpec(memory_space=pltpu.VMEM),
        scratch_shapes=[
            pltpu.VMEM((blocks, 2, rows), f32),
            pltpu.VMEM((blocks, rows), f32),
            pltpu.VMEM((blocks, 2, rows), i32),
            pltpu.VMEM((blocks, rows), i32),
            pltpu.VMEM((1, steps), i32),
            pltpu.VMEM((1, steps), f32),
            pltpu.VMEM((1, 2), i32),
            pltpu.VMEM((n, 2, tall, LANES), f32),
            pltpu.VMEM((n * FINE * tall, LANES), f32),
            pltpu.VMEM((n * FINE * tall, LANES), f32),
            pltpu.VMEM((n * COARSE * tall, LANES), f32),
            pltpu.VMEM((n * COARSE * tall, LANES), f32),
            pltpu.VMEM((n, tall, LANES), f32),
            pltpu.VMEM((n, tall, LANES), f32),
            pltpu.VMEM((n, tall, LANES), f32),
            pltpu.VMEM((nf, share, P_SIZE), f32),
            pltpu.VMEM((nf, share, P_SIZE), f32),
            pltpu.SemaphoreType.DMA((7,)),
            pltpu.SemaphoreType.DMA((n,)),
            pltpu.SemaphoreType.DMA((n,)),
            pltpu.SemaphoreType.DMA((nf,)),
            pltpu.SemaphoreType.DMA((nf,)),
        ],
        compiler_params=pltpu.CompilerParams(
            collective_id=0, has_side_effects=True, vmem_limit_bytes=62 * 1024 * 1024
        ),
        name="facet_image",
    )(visibilities, weights, uv_cells, flags, plan.reshape(1, steps), beam, facets)


def solution(mesh):
    n, nf = mesh.shape["facet"], mesh.shape["freq"]
    in_specs = (
        P("facet", None, "freq"),
        P("facet", "freq"),
        P("facet", None, "freq"),
        P("facet", "freq"),
        P(),
        P("facet", None),
        P("facet", None),
    )
    out_specs = P("facet", "freq", None)

    def whole(visibilities, *others):
        scale = 2.0 / math.sqrt(visibilities.shape[0] * visibilities.shape[2])
        return jax.shard_map(
            functools.partial(body, n, nf, scale),
            mesh=mesh, in_specs=in_specs, out_specs=out_specs, check_vma=False,
        )(visibilities, *others)

    return whole
```

```python
import functools
import math

import jax
import jax.numpy as jnp
from jax import lax
from jax.experimental import pallas as pl
from jax.experimental.pallas import tpu as pltpu
from jax.sharding import PartitionSpec as P

P_SIZE = 128
IMG = 32768
KEEP = 256
LANES = 128
HALF = P_SIZE // 2
FINE = 16
COARSE = P_SIZE // FINE
MESH = pl.DeviceIdType.MESH
NT = (((1,), (1,)), ((), ()))


def cos_sin(x):
    q = x * x
    s = jnp.full_like(q, -1.0 / math.factorial(11))
    for order in (9, 7, 5, 3, 1):
        s = s * q + (-1.0) ** (order // 2) / math.factorial(order)
    c = jnp.full_like(q, 1.0 / math.factorial(12))
    for order in (10, 8, 6, 4, 2, 0):
        c = c * q + (-1.0) ** (order // 2) / math.factorial(order)
    return c, s * x


def times(a, b):
    return a[0] * b[0] - a[1] * b[1], a[0] * b[1] + a[1] * b[0]


def square(a):
    return a[0] * a[0] - a[1] * a[1], 2.0 * (a[0] * a[1])


def powers(z, count):
    found = [None, z]
    for k in range(2, count):
        half = found[k // 2]
        found.append(square(half) if k % 2 == 0 else times(found[k // 2 + 1], half))
    return found


def partner(me, j, n):
    assert n >= 4 and n & (n - 1) == 0
    found, bit = 0, 1
    while bit < n:
        own = lax.rem(me // bit, 2)
        found = found + bit * (1 - own if j & bit else own)
        bit *= 2
    return found


def arrival_groups(n):
    return [(0, 1)] + [(lo, hi) for lo, hi in ((1, n // 2), (n // 2, n - n // 4), (n - n // 4, n))]


def kept_rows(flags):
    blocks, rows = flags.shape
    pieces = [flags[:, j * LANES:(j + 1) * LANES] for j in range(rows // LANES)]
    stacked = jnp.concatenate(pieces, axis=0)
    lower = lax.broadcasted_iota(jnp.int32, (LANES, LANES), 1) <= lax.broadcasted_iota(
        jnp.int32, (LANES, LANES), 0
    )
    inside = lax.dot_general(
        stacked.astype(jnp.bfloat16),
        jnp.where(lower, 1.0, 0.0).astype(jnp.bfloat16),
        NT,
        preferred_element_type=jnp.float32,
    )
    totals = jnp.sum(stacked, axis=1, keepdims=True)
    before = jnp.zeros((blocks, 1), jnp.float32)
    places = []
    for j, piece in enumerate(pieces):
        own = slice(j * blocks, (j + 1) * blocks)
        places.append(jnp.where(piece > 0.5, inside[own] + before - 1.0, -1.0))
        before = before + totals[own]
    return jnp.concatenate(places, axis=1)


def split3(x):
    high = x.astype(jnp.bfloat16).astype(jnp.float32)
    rest = x - high
    middle = rest.astype(jnp.bfloat16).astype(jnp.float32)
    low = rest - middle
    return jnp.concatenate([high, middle, low, jnp.zeros_like(x)], axis=0).astype(jnp.bfloat16)


def kernel(
    n, nf, scale,
    vis_hbm, w_hbm, uv_hbm, flags_hbm, plan_hbm, beam_hbm, facets_hbm,
    out_ref,
    vis, wts, uv, flg, plan, beam, facets,
    buf, fine_c, fine_s, outer_c, outer_s, half_c, half_s, amp, stage, rbuf,
    in_sem, send_sem, recv_sem, rsend_sem, rrecv_sem,
):
    mf = lax.axis_index("freq")
    me = lax.axis_index("facet")
    barrier = pltpu.get_barrier_semaphore()
    loads = [
        pltpu.make_async_copy(src, dst, in_sem.at[k])
        for k, (src, dst) in enumerate(
            [(flags_hbm, flg), (vis_hbm, vis), (w_hbm, wts), (uv_hbm, uv),
             (plan_hbm, plan), (beam_hbm, beam), (facets_hbm, facets)]
        )
    ]
    for load in loads:
        load.start()
    peers = [partner(me, j, n) for j in range(n)]
    for j in reversed(range(1, n)):
        pl.semaphore_signal(barrier, inc=1, device_id={"facet": peers[j]}, device_id_type=MESH)
    for j in range(1, nf):
        pl.semaphore_signal(
            barrier, inc=1, device_id={"freq": lax.rem(mf + j, nf)}, device_id_type=MESH
        )
    for load in loads[:4]:
        load.wait()

    flags = flg[...].astype(jnp.float32)
    place = kept_rows(flags).astype(jnp.int32)
    live = wts[...] * flags
    blocks, rows = flags.shape
    per_block = KEEP // LANES
    four = blocks * per_block
    slot_at = lax.broadcasted_iota(jnp.int32, (KEEP, rows), 0)
    for b in range(blocks):
        chosen = jnp.where(place[b:b + 1, :] == slot_at, 1.0, 0.0).astype(jnp.bfloat16)
        values = jnp.concatenate([vis[b] * live[b:b + 1, :], uv[b].astype(jnp.float32)], axis=0)
        packed = lax.dot_general(split3(values), chosen, NT, preferred_element_type=jnp.float32)
        packed = packed[0:4] + packed[4:8] + packed[8:12]
        for q in range(4):
            for h in range(per_block):
                row = (q % 2) * four + b * per_block + h
                buf[0, q // 2, row:row + 1, :] = packed[q:q + 1, h * LANES:(h + 1) * LANES]

    pl.semaphore_wait(barrier, n - 1 + nf - 1)
    sends = [
        pltpu.make_async_remote_copy(
            src_ref=buf.at[0],
            dst_ref=buf.at[j],
            send_sem=send_sem.at[j],
            recv_sem=recv_sem.at[j],
            device_id={"facet": peers[j]},
            device_id_type=MESH,
        )
        for j in range(1, n)
    ]
    for send in reversed(sends):
        send.start()

    for load in loads[4:]:
        load.wait()

    tall = 2 * four
    steps = plan.shape[1]
    row_at = lax.broadcasted_iota(jnp.int32, (tall, steps), 0)
    local = sum(
        jnp.where((row_at >= h * four + b * per_block) & (row_at < h * four + (b + 1) * per_block), b, 0)
        for h in range(2) for b in range(1, blocks)
    )
    read = plan[...] - local
    gain = beam[...] * scale
    gains = [
        jnp.sum(jnp.where(read == peers[j] * blocks, gain, 0.0), axis=1, keepdims=True)
        for j in range(n)
    ]

    high_row = lax.broadcasted_iota(jnp.int32, (tall, LANES), 0) < four
    first = facets[...] * P_SIZE - IMG // 2
    factor = jnp.where(high_row, 2 * first[:, 0:1] + (P_SIZE - 1), 2 * first[:, 1:2])
    sign = jnp.where(high_row, -1.0, 1.0)

    def swap(x):
        return jnp.concatenate([x[:, four:], x[:, :four]], axis=1)

    def tabulate(lo, hi):
        count = hi - lo
        cells = buf[lo:hi, 1]
        half = cos_sin(cells * (math.pi / IMG))
        turns = cells.astype(jnp.int32) * factor[None]
        turns = turns + swap(turns)
        turns = ((turns + IMG) & (2 * IMG - 1)) - IMG
        base = square(cos_sin(turns.astype(jnp.float32) * (math.pi / (2 * IMG))))
        x = buf[lo:hi, 0] * jnp.stack(
            [jnp.broadcast_to(gains[j], (tall, LANES)) for j in range(lo, hi)]
        )
        amp[lo:hi] = x * base[0] + swap(x) * (base[1] * sign[None])
        half_c[lo:hi] = half[0]
        half_s[lo:hi] = half[1]
        z = square(half)
        one = (jnp.ones_like(z[0]), jnp.zeros_like(z[0]))
        fine = powers(z, FINE)
        fine[0] = one
        outer = powers(square(fine[FINE // 2]), COARSE)
        outer[0] = one
        for refs, table in (((fine_c, fine_s), fine), ((outer_c, outer_s), outer)):
            for part in range(2):
                for k, entry in enumerate(table):
                    for i in range(count):
                        at = ((lo + i) * len(table) + k) * tall
                        refs[part][at:at + tall, :] = entry[part][i]

    def image_terms(slot, sums):
        cu, su, re, im = [], [], [], []
        for r in range(four):
            def pick(row):
                at = pl.ds(slot * (FINE * tall) + row, FINE, stride=tall)
                return fine_c[at, :], fine_s[at, :]

            def line(refs, row):
                return refs[0][slot, row:row + 1, :], refs[1][slot, row:row + 1, :]

            def outer_line(k, row):
                at = pl.ds(slot * (COARSE * tall) + k * tall + row, 1)
                return outer_c[at, :], outer_s[at, :]

            u = times(line((half_c, half_s), r), pick(r))
            v = times(
                (amp[slot, r:r + 1, :], amp[slot, four + r:four + r + 1, :]),
                pick(four + r),
            )
            left = [u] + [times(outer_line(k, r), u) for k in range(1, HALF // FINE)]
            right = [v] + [times(outer_line(k, four + r), v) for k in range(1, COARSE)]
            for kept, table, part in ((cu, left, 0), (su, left, 1), (re, right, 0), (im, right, 1)):
                kept.append(
                    jnp.concatenate([entry[part] for entry in table], axis=0).astype(jnp.bfloat16)
                )
        cu, su, re, im = (jnp.concatenate(kept, axis=1) for kept in (cu, su, re, im))
        return (
            sums[0] + lax.dot_general(cu, re, NT, preferred_element_type=jnp.float32),
            sums[1] + lax.dot_general(su, im, NT, preferred_element_type=jnp.float32),
        )

    sums = (jnp.zeros((HALF, P_SIZE), jnp.float32),) * 2
    for lo, hi in arrival_groups(n):
        for j in range(max(lo, 1), hi):
            sends[j - 1].wait_recv()
        tabulate(lo, hi)
        sums = lax.fori_loop(lo, hi, image_terms, sums, unroll=hi - lo if hi - lo <= 4 else 1)
    even, odd = sums

    share = P_SIZE // nf
    for f in range(nf):
        if f < nf // 2:
            at = (nf // 2 - 1 - f) * share
            stage[f] = even[at:at + share] + odd[at:at + share]
        else:
            at = (f - nf // 2) * share
            stage[f] = even[at:at + share] - odd[at:at + share]
    exchanges = []
    for j in range(1, nf):
        to = lax.rem(mf + j, nf)
        exchanges.append(
            pltpu.make_async_remote_copy(
                src_ref=stage.at[to],
                dst_ref=rbuf.at[j],
                send_sem=rsend_sem.at[j],
                recv_sem=rrecv_sem.at[j],
                device_id={"freq": to},
                device_id_type=MESH,
            )
        )
        exchanges[-1].start()
    total = stage[mf]
    for j in range(1, nf):
        exchanges[j - 1].wait_recv()
        total = total + rbuf[j]

    row8 = lax.broadcasted_iota(jnp.int32, (8, P_SIZE), 0)
    mirrored = []
    for k in reversed(range(share // 8)):
        y = pltpu.roll(total[k * 8:(k + 1) * 8], 4, 0)
        y = jnp.where((row8 & 2) != 0, pltpu.roll(y, 2, 0), pltpu.roll(y, 6, 0))
        y = jnp.where((row8 & 1) != 0, pltpu.roll(y, 1, 0), pltpu.roll(y, 7, 0))
        mirrored.append(y)
    mirrored = jnp.concatenate(mirrored, axis=0)
    out_ref[0] = jnp.where(mf < nf // 2, mirrored, total)
    for copy in sends + exchanges:
        copy.wait_send()


def body(n, nf, scale, visibilities, weights, uv_cells, flags, plan, beam, facets):
    blocks, _, rows = visibilities.shape
    four = blocks * (KEEP // LANES)
    tall = 2 * four
    share = P_SIZE // nf
    steps = plan.shape[0]
    f32, i32 = jnp.float32, jnp.int32
    return pl.pallas_call(
        functools.partial(kernel, n, nf, scale),
        out_shape=pltpu.VMEM((1, share, P_SIZE), f32),
        in_specs=[pl.BlockSpec(memory_space=pltpu.HBM)] * 7,
        out_specs=pl.BlockSpec(memory_space=pltpu.VMEM),
        scratch_shapes=[
            pltpu.VMEM((blocks, 2, rows), f32),
            pltpu.VMEM((blocks, rows), f32),
            pltpu.VMEM((blocks, 2, rows), i32),
            pltpu.VMEM((blocks, rows), i32),
            pltpu.VMEM((1, steps), i32),
            pltpu.VMEM((1, steps), f32),
            pltpu.VMEM((1, 2), i32),
            pltpu.VMEM((n, 2, tall, LANES), f32),
            pltpu.VMEM((n * FINE * tall, LANES), f32),
            pltpu.VMEM((n * FINE * tall, LANES), f32),
            pltpu.VMEM((n * COARSE * tall, LANES), f32),
            pltpu.VMEM((n * COARSE * tall, LANES), f32),
            pltpu.VMEM((n, tall, LANES), f32),
            pltpu.VMEM((n, tall, LANES), f32),
            pltpu.VMEM((n, tall, LANES), f32),
            pltpu.VMEM((nf, share, P_SIZE), f32),
            pltpu.VMEM((nf, share, P_SIZE), f32),
            pltpu.SemaphoreType.DMA((7,)),
            pltpu.SemaphoreType.DMA((n,)),
            pltpu.SemaphoreType.DMA((n,)),
            pltpu.SemaphoreType.DMA((nf,)),
            pltpu.SemaphoreType.DMA((nf,)),
        ],
        compiler_params=pltpu.CompilerParams(
            collective_id=0, has_side_effects=True, vmem_limit_bytes=62 * 1024 * 1024
        ),
        name="facet_image",
    )(visibilities, weights, uv_cells, flags, plan.reshape(1, steps), beam, facets)


def solution(mesh):
    n, nf = mesh.shape["facet"], mesh.shape["freq"]
    in_specs = (
        P("facet", None, "freq"),
        P("facet", "freq"),
        P("facet", None, "freq"),
        P("facet", "freq"),
        P(),
        P("facet", None),
        P("facet", None),
    )
    out_specs = P("facet", "freq", None)

    def whole(visibilities, *others):
        scale = 2.0 / math.sqrt(visibilities.shape[0] * visibilities.shape[2])
        return jax.shard_map(
            functools.partial(body, n, nf, scale),
            mesh=mesh, in_specs=in_specs, out_specs=out_specs, check_vma=False,
        )(visibilities, *others)

    return whole
```

```python
import functools
import math

import jax
import jax.numpy as jnp
from jax import lax
from jax.experimental import pallas as pl
from jax.experimental.pallas import tpu as pltpu
from jax.sharding import PartitionSpec as P

P_SIZE = 128
IMG = 32768
KEEP = 256
LANES = 128
HALF = P_SIZE // 2
FINE = 16
COARSE = P_SIZE // FINE
MESH = pl.DeviceIdType.MESH
NT = (((1,), (1,)), ((), ()))


def cos_sin(x):
    q = x * x
    s = jnp.full_like(q, -1.0 / math.factorial(11))
    for order in (9, 7, 5, 3, 1):
        s = s * q + (-1.0) ** (order // 2) / math.factorial(order)
    c = jnp.full_like(q, 1.0 / math.factorial(12))
    for order in (10, 8, 6, 4, 2, 0):
        c = c * q + (-1.0) ** (order // 2) / math.factorial(order)
    return c, s * x


def times(a, b):
    return a[0] * b[0] - a[1] * b[1], a[0] * b[1] + a[1] * b[0]


def square(a):
    return a[0] * a[0] - a[1] * a[1], 2.0 * (a[0] * a[1])


def powers(z, count):
    found = [None, z]
    for k in range(2, count):
        half = found[k // 2]
        found.append(square(half) if k % 2 == 0 else times(found[k // 2 + 1], half))
    return found


def partner(me, j, n):
    assert n >= 4 and n & (n - 1) == 0
    found, bit = 0, 1
    while bit < n:
        own = lax.rem(me // bit, 2)
        found = found + bit * (1 - own if j & bit else own)
        bit *= 2
    return found


def arrival_groups(n):
    return [(0, 1)] + [(lo, hi) for lo, hi in ((1, n // 2), (n // 2, n))]


def kept_rows(flags):
    blocks, rows = flags.shape
    pieces = [flags[:, j * LANES:(j + 1) * LANES] for j in range(rows // LANES)]
    stacked = jnp.concatenate(pieces, axis=0)
    lower = lax.broadcasted_iota(jnp.int32, (LANES, LANES), 1) <= lax.broadcasted_iota(
        jnp.int32, (LANES, LANES), 0
    )
    inside = lax.dot_general(
        stacked.astype(jnp.bfloat16),
        jnp.where(lower, 1.0, 0.0).astype(jnp.bfloat16),
        NT,
        preferred_element_type=jnp.float32,
    )
    totals = jnp.sum(stacked, axis=1, keepdims=True)
    before = jnp.zeros((blocks, 1), jnp.float32)
    places = []
    for j, piece in enumerate(pieces):
        own = slice(j * blocks, (j + 1) * blocks)
        places.append(jnp.where(piece > 0.5, inside[own] + before - 1.0, -1.0))
        before = before + totals[own]
    return jnp.concatenate(places, axis=1)


def split3(x):
    high = x.astype(jnp.bfloat16).astype(jnp.float32)
    rest = x - high
    middle = rest.astype(jnp.bfloat16).astype(jnp.float32)
    low = rest - middle
    pieces = [high, middle, low]
    if x.shape[0] % 16:
        pieces.append(jnp.zeros_like(x))
    return jnp.concatenate(pieces, axis=0).astype(jnp.bfloat16)


def kernel(
    n, nf, scale,
    vis_hbm, w_hbm, uv_hbm, flags_hbm, plan_hbm, beam_hbm, facets_hbm,
    out_ref,
    vis, wts, uv, flg, plan, beam, facets,
    buf, fine_c, fine_s, outer_c, outer_s, half_c, half_s, amp, stage, rbuf,
    in_sem, send_sem, recv_sem, rsend_sem, rrecv_sem,
):
    mf = lax.axis_index("freq")
    me = lax.axis_index("facet")
    barrier = pltpu.get_barrier_semaphore()
    loads = [
        pltpu.make_async_copy(src, dst, in_sem.at[k])
        for k, (src, dst) in enumerate(
            [(flags_hbm, flg), (vis_hbm, vis), (w_hbm, wts), (uv_hbm, uv),
             (plan_hbm, plan), (beam_hbm, beam), (facets_hbm, facets)]
        )
    ]
    for load in loads:
        load.start()
    peers = [partner(me, j, n) for j in range(n)]
    for j in reversed(range(1, n)):
        pl.semaphore_signal(barrier, inc=1, device_id={"facet": peers[j]}, device_id_type=MESH)
    for j in range(1, nf):
        pl.semaphore_signal(
            barrier, inc=1, device_id={"freq": lax.rem(mf + j, nf)}, device_id_type=MESH
        )
    for load in loads[:4]:
        load.wait()

    flags = flg[...].astype(jnp.float32)
    place = kept_rows(flags).astype(jnp.int32)
    live = wts[...] * flags
    blocks, rows = flags.shape
    per_block = KEEP // LANES
    four = blocks * per_block
    slot_at = lax.broadcasted_iota(jnp.int32, (KEEP, rows), 0)
    for b in range(blocks):
        chosen = jnp.where(place[b:b + 1, :] == slot_at, 1.0, 0.0).astype(jnp.bfloat16)
        values = jnp.concatenate([vis[b] * live[b:b + 1, :], uv[b].astype(jnp.float32)], axis=0)
        packed = lax.dot_general(split3(values), chosen, NT, preferred_element_type=jnp.float32)
        packed = packed[0:4] + packed[4:8] + packed[8:12]
        for q in range(4):
            for h in range(per_block):
                row = (q % 2) * four + b * per_block + h
                buf[0, q // 2, row:row + 1, :] = packed[q:q + 1, h * LANES:(h + 1) * LANES]

    pl.semaphore_wait(barrier, n - 1 + nf - 1)
    sends = [
        pltpu.make_async_remote_copy(
            src_ref=buf.at[0],
            dst_ref=buf.at[j],
            send_sem=send_sem.at[j],
            recv_sem=recv_sem.at[j],
            device_id={"facet": peers[j]},
            device_id_type=MESH,
        )
        for j in range(1, n)
    ]
    for send in reversed(sends):
        send.start()

    for load in loads[4:]:
        load.wait()

    tall = 2 * four
    steps = plan.shape[1]
    row_at = lax.broadcasted_iota(jnp.int32, (tall, steps), 0)
    local = sum(
        jnp.where((row_at >= h * four + b * per_block) & (row_at < h * four + (b + 1) * per_block), b, 0)
        for h in range(2) for b in range(1, blocks)
    )
    read = plan[...] - local
    gain = beam[...] * scale
    gains = [
        jnp.sum(jnp.where(read == peers[j] * blocks, gain, 0.0), axis=1, keepdims=True)
        for j in range(n)
    ]

    high_row = lax.broadcasted_iota(jnp.int32, (tall, LANES), 0) < four
    first = facets[...] * P_SIZE - IMG // 2
    factor = jnp.where(high_row, 2 * first[:, 0:1], 2 * first[:, 1:2] + (P_SIZE - 1))
    sign = jnp.where(high_row, -1.0, 1.0)

    def swap(x):
        return jnp.concatenate([x[:, four:], x[:, :four]], axis=1)

    def tabulate(lo, hi):
        count = hi - lo
        cells = buf[lo:hi, 1]
        half = cos_sin(cells * (math.pi / IMG))
        turns = cells.astype(jnp.int32) * factor[None]
        turns = turns + swap(turns)
        turns = ((turns + IMG) & (2 * IMG - 1)) - IMG
        base = square(cos_sin(turns.astype(jnp.float32) * (math.pi / (2 * IMG))))
        x = buf[lo:hi, 0] * jnp.stack(
            [jnp.broadcast_to(gains[j], (tall, LANES)) for j in range(lo, hi)]
        )
        amp[lo:hi] = x * base[0] + swap(x) * (base[1] * sign[None])
        half_c[lo:hi] = half[0]
        half_s[lo:hi] = half[1]
        z = square(half)
        one = (jnp.ones_like(z[0]), jnp.zeros_like(z[0]))
        fine = powers(z, FINE)
        fine[0] = one
        outer = powers(square(fine[FINE // 2]), COARSE)
        outer[0] = one
        for refs, table in (((fine_c, fine_s), fine), ((outer_c, outer_s), outer)):
            for part in range(2):
                for k, entry in enumerate(table):
                    for i in range(count):
                        at = ((lo + i) * len(table) + k) * tall
                        refs[part][at:at + tall, :] = entry[part][i]

    def image_terms(slot, sums):
        re, im, cv, sv = [], [], [], []
        for r in range(four):
            def pick(row):
                at = pl.ds(slot * (FINE * tall) + row, FINE, stride=tall)
                return fine_c[at, :], fine_s[at, :]

            def line(refs, row):
                return refs[0][slot, row:row + 1, :], refs[1][slot, row:row + 1, :]

            def outer_line(k, row):
                at = pl.ds(slot * (COARSE * tall) + k * tall + row, 1)
                return outer_c[at, :], outer_s[at, :]

            u = times(
                (amp[slot, r:r + 1, :], amp[slot, four + r:four + r + 1, :]), pick(r)
            )
            v = times(line((half_c, half_s), four + r), pick(four + r))
            left = [u] + [times(outer_line(k, r), u) for k in range(1, COARSE)]
            right = [v] + [times(outer_line(k, four + r), v) for k in range(1, HALF // FINE)]
            for kept, table, part in ((re, left, 0), (im, left, 1), (cv, right, 0), (sv, right, 1)):
                kept.append(
                    jnp.concatenate([entry[part] for entry in table], axis=0).astype(jnp.bfloat16)
                )
        re, im, cv, sv = (jnp.concatenate(kept, axis=1) for kept in (re, im, cv, sv))
        return (
            sums[0] + lax.dot_general(re, cv, NT, preferred_element_type=jnp.float32),
            sums[1] + lax.dot_general(im, sv, NT, preferred_element_type=jnp.float32),
        )

    sums = (jnp.zeros((P_SIZE, HALF), jnp.float32),) * 2
    for lo, hi in arrival_groups(n):
        for j in range(max(lo, 1), hi):
            sends[j - 1].wait_recv()
        tabulate(lo, hi)
        sums = lax.fori_loop(lo, hi, image_terms, sums, unroll=hi - lo if hi - lo <= 4 else 1)
    even, odd = sums

    share = P_SIZE // nf
    stage[...] = jnp.concatenate([even - odd, even + odd], axis=1).reshape(nf, share, P_SIZE)
    exchanges = []
    for j in range(1, nf):
        to = lax.rem(mf + j, nf)
        exchanges.append(
            pltpu.make_async_remote_copy(
                src_ref=stage.at[to],
                dst_ref=rbuf.at[j],
                send_sem=rsend_sem.at[j],
                recv_sem=rrecv_sem.at[j],
                device_id={"freq": to},
                device_id_type=MESH,
            )
        )
        exchanges[-1].start()
    total = stage[mf]
    for j in range(1, nf):
        exchanges[j - 1].wait_recv()
        total = total + rbuf[j]

    goal = lax.broadcasted_iota(jnp.int32, (P_SIZE, P_SIZE), 0)
    origin = jnp.where(goal < HALF, P_SIZE - 1 - goal, goal - HALF)
    moves = origin == lax.broadcasted_iota(jnp.int32, (P_SIZE, P_SIZE), 1)
    moved = lax.dot_general(
        split3(total), jnp.where(moves, 1.0, 0.0).astype(jnp.bfloat16), NT,
        preferred_element_type=jnp.float32,
    )
    out_ref[0] = moved[:share] + moved[share:2 * share] + moved[2 * share:3 * share]
    for copy in sends + exchanges:
        copy.wait_send()


def body(n, nf, scale, visibilities, weights, uv_cells, flags, plan, beam, facets):
    blocks, _, rows = visibilities.shape
    four = blocks * (KEEP // LANES)
    tall = 2 * four
    share = P_SIZE // nf
    steps = plan.shape[0]
    f32, i32 = jnp.float32, jnp.int32
    return pl.pallas_call(
        functools.partial(kernel, n, nf, scale),
        out_shape=pltpu.VMEM((1, share, P_SIZE), f32),
        in_specs=[pl.BlockSpec(memory_space=pltpu.HBM)] * 7,
        out_specs=pl.BlockSpec(memory_space=pltpu.VMEM),
        scratch_shapes=[
            pltpu.VMEM((blocks, 2, rows), f32),
            pltpu.VMEM((blocks, rows), f32),
            pltpu.VMEM((blocks, 2, rows), i32),
            pltpu.VMEM((blocks, rows), i32),
            pltpu.VMEM((1, steps), i32),
            pltpu.VMEM((1, steps), f32),
            pltpu.VMEM((1, 2), i32),
            pltpu.VMEM((n, 2, tall, LANES), f32),
            pltpu.VMEM((n * FINE * tall, LANES), f32),
            pltpu.VMEM((n * FINE * tall, LANES), f32),
            pltpu.VMEM((n * COARSE * tall, LANES), f32),
            pltpu.VMEM((n * COARSE * tall, LANES), f32),
            pltpu.VMEM((n, tall, LANES), f32),
            pltpu.VMEM((n, tall, LANES), f32),
            pltpu.VMEM((n, tall, LANES), f32),
            pltpu.VMEM((nf, share, P_SIZE), f32),
            pltpu.VMEM((nf, share, P_SIZE), f32),
            pltpu.SemaphoreType.DMA((7,)),
            pltpu.SemaphoreType.DMA((n,)),
            pltpu.SemaphoreType.DMA((n,)),
            pltpu.SemaphoreType.DMA((nf,)),
            pltpu.SemaphoreType.DMA((nf,)),
        ],
        compiler_params=pltpu.CompilerParams(
            collective_id=0, has_side_effects=True, vmem_limit_bytes=62 * 1024 * 1024
        ),
        name="facet_image",
    )(visibilities, weights, uv_cells, flags, plan.reshape(1, steps), beam, facets)


def solution(mesh):
    n, nf = mesh.shape["facet"], mesh.shape["freq"]
    in_specs = (
        P("facet", None, "freq"),
        P("facet", "freq"),
        P("facet", None, "freq"),
        P("facet", "freq"),
        P(),
        P("facet", None),
        P("facet", None),
    )
    out_specs = P("facet", "freq", None)

    def whole(visibilities, *others):
        scale = 2.0 / math.sqrt(visibilities.shape[0] * visibilities.shape[2])
        return jax.shard_map(
            functools.partial(body, n, nf, scale),
            mesh=mesh, in_specs=in_specs, out_specs=out_specs, check_vma=False,
        )(visibilities, *others)

    return whole
```

```python
import functools
import math

import jax
import jax.numpy as jnp
from jax import lax
from jax.experimental import pallas as pl
from jax.experimental.pallas import tpu as pltpu
from jax.sharding import PartitionSpec as P

P_SIZE = 128
IMG = 32768
KEEP = 256
LANES = 128
HALF = P_SIZE // 2
FINE = 8
MESH = pl.DeviceIdType.MESH
NT = (((1,), (1,)), ((), ()))


def cos_sin(x):
    q = x * x
    s = jnp.full_like(q, -1.0 / math.factorial(11))
    for order in (9, 7, 5, 3, 1):
        s = s * q + (-1.0) ** (order // 2) / math.factorial(order)
    c = jnp.full_like(q, 1.0 / math.factorial(12))
    for order in (10, 8, 6, 4, 2, 0):
        c = c * q + (-1.0) ** (order // 2) / math.factorial(order)
    return c, s * x


def times(a, b):
    return a[0] * b[0] - a[1] * b[1], a[0] * b[1] + a[1] * b[0]


def square(a):
    return a[0] * a[0] - a[1] * a[1], 2.0 * (a[0] * a[1])


def powers(z, count):
    found = [None, z]
    for k in range(2, count):
        half = found[k // 2]
        found.append(square(half) if k % 2 == 0 else times(found[k // 2 + 1], half))
    return found


def partner(me, j, n):
    assert n & (n - 1) == 0
    found, bit = 0, 1
    while bit < n:
        own = lax.rem(me // bit, 2)
        found = found + bit * (1 - own if j & bit else own)
        bit *= 2
    return found


def arrival_groups(n):
    return [(0, 1)] + [(lo, hi) for lo, hi in ((1, n // 2), (n // 2, n)) if lo < hi]


def kept_rows(flags):
    blocks, rows = flags.shape
    pieces = [flags[:, j * LANES:(j + 1) * LANES] for j in range(rows // LANES)]
    stacked = jnp.concatenate(pieces, axis=0)
    lower = lax.broadcasted_iota(jnp.int32, (LANES, LANES), 1) <= lax.broadcasted_iota(
        jnp.int32, (LANES, LANES), 0
    )
    inside = lax.dot_general(
        stacked.astype(jnp.bfloat16),
        jnp.where(lower, 1.0, 0.0).astype(jnp.bfloat16),
        NT,
        preferred_element_type=jnp.float32,
    )
    totals = jnp.sum(stacked, axis=1, keepdims=True)
    before = jnp.zeros((blocks, 1), jnp.float32)
    places = []
    for j, piece in enumerate(pieces):
        own = slice(j * blocks, (j + 1) * blocks)
        places.append(jnp.where(piece > 0.5, inside[own] + before - 1.0, -1.0))
        before = before + totals[own]
    return jnp.concatenate(places, axis=1)


def split3(x):
    high = x.astype(jnp.bfloat16).astype(jnp.float32)
    rest = x - high
    middle = rest.astype(jnp.bfloat16).astype(jnp.float32)
    low = rest - middle
    return jnp.concatenate([high, middle, low, jnp.zeros_like(x)], axis=0).astype(jnp.bfloat16)


def kernel(
    n, nf, scale,
    vis_hbm, w_hbm, uv_hbm, flags_hbm, plan_hbm, beam_hbm, facets_hbm,
    out_ref,
    vis, wts, uv, flg, plan, beam, facets,
    buf, fine_c, fine_s, step_c, step_s, half_c, half_s, amp, stage, rbuf,
    in_sem, send_sem, recv_sem, rsend_sem, rrecv_sem,
):
    mf = lax.axis_index("freq")
    me = lax.axis_index("facet")
    barrier = pltpu.get_barrier_semaphore()
    loads = [
        pltpu.make_async_copy(src, dst, in_sem.at[k])
        for k, (src, dst) in enumerate(
            [(flags_hbm, flg), (vis_hbm, vis), (w_hbm, wts), (uv_hbm, uv),
             (plan_hbm, plan), (beam_hbm, beam), (facets_hbm, facets)]
        )
    ]
    for j in range(1, nf):
        pl.semaphore_signal(
            barrier, inc=1, device_id={"freq": lax.rem(mf + j, nf)}, device_id_type=MESH
        )
    peers = [partner(me, j, n) for j in range(n)]
    for j in reversed(range(1, n)):
        pl.semaphore_signal(barrier, inc=1, device_id={"facet": peers[j]}, device_id_type=MESH)
    for load in loads:
        load.start()
    for load in loads[:4]:
        load.wait()

    flags = flg[...].astype(jnp.float32)
    place = kept_rows(flags).astype(jnp.int32)
    live = wts[...] * flags
    blocks, rows = flags.shape
    per_block = KEEP // LANES
    four = blocks * per_block
    slot_at = lax.broadcasted_iota(jnp.int32, (KEEP, rows), 0)
    for b in range(blocks):
        chosen = jnp.where(place[b:b + 1, :] == slot_at, 1.0, 0.0).astype(jnp.bfloat16)
        values = jnp.concatenate([vis[b] * live[b:b + 1, :], uv[b].astype(jnp.float32)], axis=0)
        packed = lax.dot_general(split3(values), chosen, NT, preferred_element_type=jnp.float32)
        packed = packed[0:4] + packed[4:8] + packed[8:12]
        for q in range(4):
            for h in range(per_block):
                row = (q % 2) * four + b * per_block + h
                buf[0, q // 2, row:row + 1, :] = packed[q:q + 1, h * LANES:(h + 1) * LANES]

    pl.semaphore_wait(barrier, n - 1 + nf - 1)
    sends = [
        pltpu.make_async_remote_copy(
            src_ref=buf.at[0],
            dst_ref=buf.at[j],
            send_sem=send_sem.at[j],
            recv_sem=recv_sem.at[j],
            device_id={"facet": peers[j]},
            device_id_type=MESH,
        )
        for j in range(1, n)
    ]
    for send in reversed(sends):
        send.start()

    for load in loads[4:]:
        load.wait()

    tall = 2 * four
    steps = plan.shape[1]
    row_at = lax.broadcasted_iota(jnp.int32, (tall, steps), 0)
    local = sum(
        jnp.where((row_at >= h * four + b * per_block) & (row_at < h * four + (b + 1) * per_block), b, 0)
        for h in range(2) for b in range(1, blocks)
    )
    read = plan[...] - local
    gain = beam[...] * scale
    gains = [
        jnp.sum(jnp.where(read == peers[j] * blocks, gain, 0.0), axis=1, keepdims=True)
        for j in range(n)
    ]

    high_row = lax.broadcasted_iota(jnp.int32, (tall, LANES), 0) < four
    first = facets[...] * P_SIZE - IMG // 2
    factor = jnp.where(high_row, 2 * first[:, 0:1] + (P_SIZE - 1), 2 * first[:, 1:2])
    sign = jnp.where(high_row, -1.0, 1.0)

    def swap(x):
        return jnp.concatenate([x[:, four:], x[:, :four]], axis=1)

    def tabulate(lo, hi):
        count = hi - lo
        cells = buf[lo:hi, 1]
        half = cos_sin(cells * (math.pi / IMG))
        turns = cells.astype(jnp.int32) * factor[None]
        turns = turns + swap(turns)
        turns = ((turns + IMG) & (2 * IMG - 1)) - IMG
        base = square(cos_sin(turns.astype(jnp.float32) * (math.pi / (2 * IMG))))
        x = buf[lo:hi, 0] * jnp.stack(
            [jnp.broadcast_to(gains[j], (tall, LANES)) for j in range(lo, hi)]
        )
        amp[lo:hi] = x * base[0] + swap(x) * (base[1] * sign[None])
        half_c[lo:hi] = half[0]
        half_s[lo:hi] = half[1]
        z = square(half)
        one = (jnp.ones_like(z[0]), jnp.zeros_like(z[0]))
        fine = powers(z, FINE)
        fine[0] = one
        step_c[lo:hi], step_s[lo:hi] = square(fine[FINE // 2])
        for ref, part in ((fine_c, 0), (fine_s, 1)):
            for k, entry in enumerate(fine):
                for i in range(count):
                    at = ((lo + i) * FINE + k) * tall
                    ref[at:at + tall, :] = entry[part][i]

    def image_terms(slot, sums):
        cu, su, re, im = [], [], [], []
        for r in range(four):
            def pick(row):
                at = pl.ds(slot * (FINE * tall) + row, FINE, stride=tall)
                return fine_c[at, :], fine_s[at, :]

            def line(refs, row):
                return refs[0][slot, row:row + 1, :], refs[1][slot, row:row + 1, :]

            def climb(start, row, rows_at):
                step = line((step_c, step_s), row)
                double = jnp.broadcast_to(step[0] + step[0], (FINE, LANES))
                table = [start, times(step, start)]
                while len(table) * FINE < rows_at:
                    table.append(
                        tuple(double * now - past for past, now in zip(table[-2], table[-1]))
                    )
                return table

            u = times(line((half_c, half_s), r), pick(r))
            v = times(
                (amp[slot, r:r + 1, :], amp[slot, four + r:four + r + 1, :]),
                pick(four + r),
            )
            left = climb(u, r, HALF)
            right = climb(v, four + r, P_SIZE)
            for kept, table, part in ((cu, left, 0), (su, left, 1), (re, right, 0), (im, right, 1)):
                kept.append(
                    jnp.concatenate([entry[part] for entry in table], axis=0).astype(jnp.bfloat16)
                )
        cu, su, re, im = (jnp.concatenate(kept, axis=1) for kept in (cu, su, re, im))
        return (
            sums[0] + lax.dot_general(cu, re, NT, preferred_element_type=jnp.float32),
            sums[1] + lax.dot_general(su, im, NT, preferred_element_type=jnp.float32),
        )

    sums = (jnp.zeros((HALF, P_SIZE), jnp.float32),) * 2
    for lo, hi in arrival_groups(n):
        for j in range(max(lo, 1), hi):
            sends[j - 1].wait_recv()
        tabulate(lo, hi)
        sums = lax.fori_loop(lo, hi, image_terms, sums, unroll=hi - lo if hi - lo <= 4 else 1)
    even, odd = sums

    share = P_SIZE // nf
    for f in range(nf):
        if f < nf // 2:
            at = (nf // 2 - 1 - f) * share
            stage[f] = even[at:at + share] + odd[at:at + share]
        else:
            at = (f - nf // 2) * share
            stage[f] = even[at:at + share] - odd[at:at + share]
    exchanges = []
    for j in range(1, nf):
        to = lax.rem(mf + j, nf)
        exchanges.append(
            pltpu.make_async_remote_copy(
                src_ref=stage.at[to],
                dst_ref=rbuf.at[j],
                send_sem=rsend_sem.at[j],
                recv_sem=rrecv_sem.at[j],
                device_id={"freq": to},
                device_id_type=MESH,
            )
        )
        exchanges[-1].start()
    total = stage[mf]
    for j in range(1, nf):
        exchanges[j - 1].wait_recv()
        total = total + rbuf[j]

    row8 = lax.broadcasted_iota(jnp.int32, (8, P_SIZE), 0)
    mirrored = []
    for k in reversed(range(share // 8)):
        y = pltpu.roll(total[k * 8:(k + 1) * 8], 4, 0)
        y = jnp.where((row8 & 2) != 0, pltpu.roll(y, 2, 0), pltpu.roll(y, 6, 0))
        y = jnp.where((row8 & 1) != 0, pltpu.roll(y, 1, 0), pltpu.roll(y, 7, 0))
        mirrored.append(y)
    mirrored = jnp.concatenate(mirrored, axis=0)
    out_ref[0] = jnp.where(mf < nf // 2, mirrored, total)
    for copy in sends + exchanges:
        copy.wait_send()


def body(n, nf, scale, visibilities, weights, uv_cells, flags, plan, beam, facets):
    blocks, _, rows = visibilities.shape
    four = blocks * (KEEP // LANES)
    tall = 2 * four
    share = P_SIZE // nf
    steps = plan.shape[0]
    f32, i32 = jnp.float32, jnp.int32
    return pl.pallas_call(
        functools.partial(kernel, n, nf, scale),
        out_shape=pltpu.VMEM((1, share, P_SIZE), f32),
        in_specs=[pl.BlockSpec(memory_space=pltpu.HBM)] * 7,
        out_specs=pl.BlockSpec(memory_space=pltpu.VMEM),
        scratch_shapes=[
            pltpu.VMEM((blocks, 2, rows), f32),
            pltpu.VMEM((blocks, rows), f32),
            pltpu.VMEM((blocks, 2, rows), i32),
            pltpu.VMEM((blocks, rows), i32),
            pltpu.VMEM((1, steps), i32),
            pltpu.VMEM((1, steps), f32),
            pltpu.VMEM((1, 2), i32),
            pltpu.VMEM((n, 2, tall, LANES), f32),
            pltpu.VMEM((n * FINE * tall, LANES), f32),
            pltpu.VMEM((n * FINE * tall, LANES), f32),
            pltpu.VMEM((n, tall, LANES), f32),
            pltpu.VMEM((n, tall, LANES), f32),
            pltpu.VMEM((n, tall, LANES), f32),
            pltpu.VMEM((n, tall, LANES), f32),
            pltpu.VMEM((n, tall, LANES), f32),
            pltpu.VMEM((nf, share, P_SIZE), f32),
            pltpu.VMEM((nf, share, P_SIZE), f32),
            pltpu.SemaphoreType.DMA((7,)),
            pltpu.SemaphoreType.DMA((n,)),
            pltpu.SemaphoreType.DMA((n,)),
            pltpu.SemaphoreType.DMA((nf,)),
            pltpu.SemaphoreType.DMA((nf,)),
        ],
        compiler_params=pltpu.CompilerParams(
            collective_id=0, has_side_effects=True, vmem_limit_bytes=62 * 1024 * 1024
        ),
        name="facet_image",
    )(visibilities, weights, uv_cells, flags, plan.reshape(1, steps), beam, facets)


def solution(mesh):
    n, nf = mesh.shape["facet"], mesh.shape["freq"]
    in_specs = (
        P("facet", None, "freq"),
        P("facet", "freq"),
        P("facet", None, "freq"),
        P("facet", "freq"),
        P(),
        P("facet", None),
        P("facet", None),
    )
    out_specs = P("facet", "freq", None)

    def whole(visibilities, *others):
        scale = 2.0 / math.sqrt(visibilities.shape[0] * visibilities.shape[2])
        return jax.shard_map(
            functools.partial(body, n, nf, scale),
            mesh=mesh, in_specs=in_specs, out_specs=out_specs, check_vma=False,
        )(visibilities, *others)

    return whole
```

```python
import functools
import math

import jax
import jax.numpy as jnp
from jax import lax
from jax.experimental import pallas as pl
from jax.experimental.pallas import tpu as pltpu
from jax.sharding import PartitionSpec as P

P_SIZE = 128
IMG = 32768
KEEP = 256
LANES = 128
HALF = P_SIZE // 2
FINE = 8
MESH = pl.DeviceIdType.MESH
NT = (((1,), (1,)), ((), ()))


def cos_sin(x):
    q = x * x
    s = jnp.full_like(q, -1.0 / math.factorial(11))
    for order in (9, 7, 5, 3, 1):
        s = s * q + (-1.0) ** (order // 2) / math.factorial(order)
    c = jnp.full_like(q, 1.0 / math.factorial(12))
    for order in (10, 8, 6, 4, 2, 0):
        c = c * q + (-1.0) ** (order // 2) / math.factorial(order)
    return c, s * x


def times(a, b):
    return a[0] * b[0] - a[1] * b[1], a[0] * b[1] + a[1] * b[0]


def square(a):
    return a[0] * a[0] - a[1] * a[1], 2.0 * (a[0] * a[1])


def powers(z, count):
    found = [None, z]
    for k in range(2, count):
        half = found[k // 2]
        found.append(square(half) if k % 2 == 0 else times(found[k // 2 + 1], half))
    return found


def partner(me, j, n):
    assert n & (n - 1) == 0
    found, bit = 0, 1
    while bit < n:
        own = lax.rem(me // bit, 2)
        found = found + bit * (1 - own if j & bit else own)
        bit *= 2
    return found


def arrival_groups(n):
    return [(0, 1), (1, n)]


def kept_rows(flags):
    blocks, rows = flags.shape
    pieces = [flags[:, j * LANES:(j + 1) * LANES] for j in range(rows // LANES)]
    stacked = jnp.concatenate(pieces, axis=0)
    lower = lax.broadcasted_iota(jnp.int32, (LANES, LANES), 1) <= lax.broadcasted_iota(
        jnp.int32, (LANES, LANES), 0
    )
    inside = lax.dot_general(
        stacked.astype(jnp.bfloat16),
        jnp.where(lower, 1.0, 0.0).astype(jnp.bfloat16),
        NT,
        preferred_element_type=jnp.float32,
    )
    totals = jnp.sum(stacked, axis=1, keepdims=True)
    before = jnp.zeros((blocks, 1), jnp.float32)
    places = []
    for j, piece in enumerate(pieces):
        own = slice(j * blocks, (j + 1) * blocks)
        places.append(jnp.where(piece > 0.5, inside[own] + before - 1.0, -1.0))
        before = before + totals[own]
    return jnp.concatenate(places, axis=1)


def split3(x):
    high = x.astype(jnp.bfloat16).astype(jnp.float32)
    rest = x - high
    middle = rest.astype(jnp.bfloat16).astype(jnp.float32)
    low = rest - middle
    return jnp.concatenate([high, middle, low, jnp.zeros_like(x)], axis=0).astype(jnp.bfloat16)


def kernel(
    n, nf, scale,
    vis_hbm, w_hbm, uv_hbm, flags_hbm, plan_hbm, beam_hbm, facets_hbm,
    out_ref,
    vis, wts, uv, flg, plan, beam, facets,
    buf, fine_c, fine_s, step_c, step_s, half_c, half_s, amp, stage, rbuf,
    in_sem, send_sem, recv_sem, rsend_sem, rrecv_sem,
):
    mf = lax.axis_index("freq")
    me = lax.axis_index("facet")
    barrier = pltpu.get_barrier_semaphore()
    loads = [
        pltpu.make_async_copy(src, dst, in_sem.at[k])
        for k, (src, dst) in enumerate(
            [(flags_hbm, flg), (vis_hbm, vis), (w_hbm, wts), (uv_hbm, uv),
             (plan_hbm, plan), (beam_hbm, beam), (facets_hbm, facets)]
        )
    ]
    for load in loads[:4]:
        load.start()
    for j in reversed(range(1, nf)):
        pl.semaphore_signal(
            barrier, inc=1, device_id={"freq": partner(mf, j, nf)}, device_id_type=MESH
        )
    peers = [partner(me, j, n) for j in range(n)]
    for j in reversed(range(1, n)):
        pl.semaphore_signal(barrier, inc=1, device_id={"facet": peers[j]}, device_id_type=MESH)
    for load in loads[4:]:
        load.start()
    loads[0].wait()
    flags = flg[...].astype(jnp.float32)
    place = kept_rows(flags).astype(jnp.int32)
    for load in loads[1:4]:
        load.wait()
    live = wts[...] * flags
    blocks, rows = flags.shape
    per_block = KEEP // LANES
    four = blocks * per_block
    slot_at = lax.broadcasted_iota(jnp.int32, (KEEP, rows), 0)
    for b in range(blocks):
        chosen = jnp.where(place[b:b + 1, :] == slot_at, 1.0, 0.0).astype(jnp.bfloat16)
        values = jnp.concatenate([vis[b] * live[b:b + 1, :], uv[b].astype(jnp.float32)], axis=0)
        packed = lax.dot_general(split3(values), chosen, NT, preferred_element_type=jnp.float32)
        packed = packed[0:4] + packed[4:8] + packed[8:12]
        for q in range(4):
            for h in range(per_block):
                row = (q % 2) * four + b * per_block + h
                buf[0, q // 2, row:row + 1, :] = packed[q:q + 1, h * LANES:(h + 1) * LANES]

    pl.semaphore_wait(barrier, n - 1 + nf - 1)
    sends = [
        pltpu.make_async_remote_copy(
            src_ref=buf.at[0],
            dst_ref=buf.at[j],
            send_sem=send_sem.at[j],
            recv_sem=recv_sem.at[j],
            device_id={"facet": peers[j]},
            device_id_type=MESH,
        )
        for j in range(1, n)
    ]
    for send in reversed(sends):
        send.start()

    for load in loads[4:]:
        load.wait()

    tall = 2 * four
    steps = plan.shape[1]
    row_at = lax.broadcasted_iota(jnp.int32, (tall, steps), 0)
    local = sum(
        jnp.where((row_at >= h * four + b * per_block) & (row_at < h * four + (b + 1) * per_block), b, 0)
        for h in range(2) for b in range(1, blocks)
    )
    read = plan[...] - local
    gain = beam[...] * scale
    gains = [
        jnp.sum(jnp.where(read == peers[j] * blocks, gain, 0.0), axis=1, keepdims=True)
        for j in range(n)
    ]

    high_row = lax.broadcasted_iota(jnp.int32, (tall, LANES), 0) < four
    first = facets[...] * P_SIZE - IMG // 2
    factor = jnp.where(high_row, 2 * first[:, 0:1] + (P_SIZE - 1), 2 * first[:, 1:2])
    sign = jnp.where(high_row, -1.0, 1.0)

    def swap(x):
        return jnp.concatenate([x[:, four:], x[:, :four]], axis=1)

    def tabulate(lo, hi):
        count = hi - lo
        cells = buf[lo:hi, 1]
        half = cos_sin(cells * (math.pi / IMG))
        turns = cells.astype(jnp.int32) * factor[None]
        turns = turns + swap(turns)
        turns = ((turns + IMG) & (2 * IMG - 1)) - IMG
        base = square(cos_sin(turns.astype(jnp.float32) * (math.pi / (2 * IMG))))
        x = buf[lo:hi, 0] * jnp.stack(
            [jnp.broadcast_to(gains[j], (tall, LANES)) for j in range(lo, hi)]
        )
        amp[lo:hi] = x * base[0] + swap(x) * (base[1] * sign[None])
        half_c[lo:hi] = half[0]
        half_s[lo:hi] = half[1]
        z = square(half)
        one = (jnp.ones_like(z[0]), jnp.zeros_like(z[0]))
        fine = powers(z, FINE)
        fine[0] = one
        step_c[lo:hi], step_s[lo:hi] = square(fine[FINE // 2])
        for ref, part in ((fine_c, 0), (fine_s, 1)):
            for k, entry in enumerate(fine):
                for i in range(count):
                    at = ((lo + i) * FINE + k) * tall
                    ref[at:at + tall, :] = entry[part][i]

    def image_terms(slot, sums):
        cu, su, re, im = [], [], [], []
        for r in range(four):
            def pick(row):
                at = pl.ds(slot * (FINE * tall) + row, FINE, stride=tall)
                return fine_c[at, :], fine_s[at, :]

            def line(refs, row):
                return refs[0][slot, row:row + 1, :], refs[1][slot, row:row + 1, :]

            def climb(start, row, rows_at):
                step = line((step_c, step_s), row)
                double = jnp.broadcast_to(step[0] + step[0], (FINE, LANES))
                table = [start, times(step, start)]
                while len(table) * FINE < rows_at:
                    table.append(
                        tuple(double * now - past for past, now in zip(table[-2], table[-1]))
                    )
                return table

            u = times(line((half_c, half_s), r), pick(r))
            v = times(
                (amp[slot, r:r + 1, :], amp[slot, four + r:four + r + 1, :]),
                pick(four + r),
            )
            left = climb(u, r, HALF)
            right = climb(v, four + r, P_SIZE)
            for kept, table, part in ((cu, left, 0), (su, left, 1), (re, right, 0), (im, right, 1)):
                kept.append(
                    jnp.concatenate([entry[part] for entry in table], axis=0).astype(jnp.bfloat16)
                )
        cu, su, re, im = (jnp.concatenate(kept, axis=1) for kept in (cu, su, re, im))
        return (
            sums[0] + lax.dot_general(cu, re, NT, preferred_element_type=jnp.float32),
            sums[1] + lax.dot_general(su, im, NT, preferred_element_type=jnp.float32),
        )

    sums = (jnp.zeros((HALF, P_SIZE), jnp.float32),) * 2
    for lo, hi in arrival_groups(n):
        for j in range(max(lo, 1), hi):
            sends[j - 1].wait_recv()
        tabulate(lo, hi)
        sums = lax.fori_loop(lo, hi, image_terms, sums, unroll=hi - lo if hi - lo <= 8 else 1)
    even, odd = sums

    share = P_SIZE // nf
    for f in range(nf):
        if f < nf // 2:
            at = (nf // 2 - 1 - f) * share
            stage[f] = even[at:at + share] + odd[at:at + share]
        else:
            at = (f - nf // 2) * share
            stage[f] = even[at:at + share] - odd[at:at + share]
    exchanges = []
    for j in reversed(range(1, nf)):
        to = partner(mf, j, nf)
        exchanges.append(
            pltpu.make_async_remote_copy(
                src_ref=stage.at[to],
                dst_ref=rbuf.at[j],
                send_sem=rsend_sem.at[j],
                recv_sem=rrecv_sem.at[j],
                device_id={"freq": to},
                device_id_type=MESH,
            )
        )
        exchanges[-1].start()
    total = stage[mf]
    for exchange in exchanges:
        exchange.wait_recv()
    for j in range(1, nf):
        total = total + rbuf[j]

    row8 = lax.broadcasted_iota(jnp.int32, (8, P_SIZE), 0)
    mirrored = []
    for k in reversed(range(share // 8)):
        y = pltpu.roll(total[k * 8:(k + 1) * 8], 4, 0)
        y = jnp.where((row8 & 2) != 0, pltpu.roll(y, 2, 0), pltpu.roll(y, 6, 0))
        y = jnp.where((row8 & 1) != 0, pltpu.roll(y, 1, 0), pltpu.roll(y, 7, 0))
        mirrored.append(y)
    mirrored = jnp.concatenate(mirrored, axis=0)
    out_ref[0] = jnp.where(mf < nf // 2, mirrored, total)
    for copy in sends + exchanges:
        copy.wait_send()


def body(n, nf, scale, visibilities, weights, uv_cells, flags, plan, beam, facets):
    blocks, _, rows = visibilities.shape
    four = blocks * (KEEP // LANES)
    tall = 2 * four
    share = P_SIZE // nf
    steps = plan.shape[0]
    f32, i32 = jnp.float32, jnp.int32
    return pl.pallas_call(
        functools.partial(kernel, n, nf, scale),
        out_shape=pltpu.VMEM((1, share, P_SIZE), f32),
        in_specs=[pl.BlockSpec(memory_space=pltpu.HBM)] * 7,
        out_specs=pl.BlockSpec(memory_space=pltpu.VMEM),
        scratch_shapes=[
            pltpu.VMEM((blocks, 2, rows), f32),
            pltpu.VMEM((blocks, rows), f32),
            pltpu.VMEM((blocks, 2, rows), i32),
            pltpu.VMEM((blocks, rows), i32),
            pltpu.VMEM((1, steps), i32),
            pltpu.VMEM((1, steps), f32),
            pltpu.VMEM((1, 2), i32),
            pltpu.VMEM((n, 2, tall, LANES), f32),
            pltpu.VMEM((n * FINE * tall, LANES), f32),
            pltpu.VMEM((n * FINE * tall, LANES), f32),
            pltpu.VMEM((n, tall, LANES), f32),
            pltpu.VMEM((n, tall, LANES), f32),
            pltpu.VMEM((n, tall, LANES), f32),
            pltpu.VMEM((n, tall, LANES), f32),
            pltpu.VMEM((n, tall, LANES), f32),
            pltpu.VMEM((nf, share, P_SIZE), f32),
            pltpu.VMEM((nf, share, P_SIZE), f32),
            pltpu.SemaphoreType.DMA((7,)),
            pltpu.SemaphoreType.DMA((n,)),
            pltpu.SemaphoreType.DMA((n,)),
            pltpu.SemaphoreType.DMA((nf,)),
            pltpu.SemaphoreType.DMA((nf,)),
        ],
        compiler_params=pltpu.CompilerParams(
            collective_id=0, has_side_effects=True, vmem_limit_bytes=62 * 1024 * 1024
        ),
        name="facet_image",
    )(visibilities, weights, uv_cells, flags, plan.reshape(1, steps), beam, facets)


def solution(mesh):
    n, nf = mesh.shape["facet"], mesh.shape["freq"]
    in_specs = (
        P("facet", None, "freq"),
        P("facet", "freq"),
        P("facet", None, "freq"),
        P("facet", "freq"),
        P(),
        P("facet", None),
        P("facet", None),
    )
    out_specs = P("facet", "freq", None)

    def whole(visibilities, *others):
        scale = 2.0 / math.sqrt(visibilities.shape[0] * visibilities.shape[2])
        return jax.shard_map(
            functools.partial(body, n, nf, scale),
            mesh=mesh, in_specs=in_specs, out_specs=out_specs, check_vma=False,
        )(visibilities, *others)

    return whole
```

```python
import functools
import math

import jax
import jax.numpy as jnp
from jax import lax
from jax.experimental import pallas as pl
from jax.experimental.pallas import tpu as pltpu
from jax.sharding import PartitionSpec as P

P_SIZE = 128
IMG = 32768
KEEP = 256
LANES = 128
HALF = P_SIZE // 2
FINE = 8
MESH = pl.DeviceIdType.MESH
NT = (((1,), (1,)), ((), ()))


def cos_sin(x):
    q = x * x
    s = jnp.full_like(q, -1.0 / math.factorial(11))
    for order in (9, 7, 5, 3, 1):
        s = s * q + (-1.0) ** (order // 2) / math.factorial(order)
    c = jnp.full_like(q, 1.0 / math.factorial(12))
    for order in (10, 8, 6, 4, 2, 0):
        c = c * q + (-1.0) ** (order // 2) / math.factorial(order)
    return c, s * x


def times(a, b):
    return a[0] * b[0] - a[1] * b[1], a[0] * b[1] + a[1] * b[0]


def square(a):
    return a[0] * a[0] - a[1] * a[1], 2.0 * (a[0] * a[1])


def powers(z, count):
    found = [None, z]
    for k in range(2, count):
        half = found[k // 2]
        found.append(square(half) if k % 2 == 0 else times(found[k // 2 + 1], half))
    return found


def partner(me, j, n):
    assert n & (n - 1) == 0
    found, bit = 0, 1
    while bit < n:
        own = lax.rem(me // bit, 2)
        found = found + bit * (1 - own if j & bit else own)
        bit *= 2
    return found


def arrival_groups(n):
    return [(0, 1), (1, n // 2), (n // 2, n - n // 4), (n - n // 4, n)]


def kept_rows(flags):
    blocks, rows = flags.shape
    pieces = [flags[:, j * LANES:(j + 1) * LANES] for j in range(rows // LANES)]
    stacked = jnp.concatenate(pieces, axis=0)
    lower = lax.broadcasted_iota(jnp.int32, (LANES, LANES), 1) <= lax.broadcasted_iota(
        jnp.int32, (LANES, LANES), 0
    )
    inside = lax.dot_general(
        stacked.astype(jnp.bfloat16),
        jnp.where(lower, 1.0, 0.0).astype(jnp.bfloat16),
        NT,
        preferred_element_type=jnp.float32,
    )
    totals = jnp.sum(stacked, axis=1, keepdims=True)
    before = jnp.zeros((blocks, 1), jnp.float32)
    places = []
    for j, piece in enumerate(pieces):
        own = slice(j * blocks, (j + 1) * blocks)
        places.append(jnp.where(piece > 0.5, inside[own] + before - 1.0, -1.0))
        before = before + totals[own]
    return jnp.concatenate(places, axis=1)


def split3(x):
    high = x.astype(jnp.bfloat16).astype(jnp.float32)
    rest = x - high
    middle = rest.astype(jnp.bfloat16).astype(jnp.float32)
    low = rest - middle
    return jnp.concatenate([high, middle, low, jnp.zeros_like(x)], axis=0).astype(jnp.bfloat16)


def kernel(
    n, nf, scale,
    vis_hbm, w_hbm, uv_hbm, flags_hbm, plan_hbm, beam_hbm, facets_hbm,
    out_ref,
    vis, wts, uv, flg, plan, beam, facets,
    buf, fine_c, fine_s, step_c, step_s, half_c, half_s, amp, stage, rbuf,
    in_sem, send_sem, recv_sem, rsend_sem, rrecv_sem,
):
    mf = lax.axis_index("freq")
    me = lax.axis_index("facet")
    barrier = pltpu.get_barrier_semaphore()
    loads = [
        pltpu.make_async_copy(src, dst, in_sem.at[k])
        for k, (src, dst) in enumerate(
            [(flags_hbm, flg), (vis_hbm, vis), (w_hbm, wts), (uv_hbm, uv),
             (plan_hbm, plan), (beam_hbm, beam), (facets_hbm, facets)]
        )
    ]
    for load in loads[:4]:
        load.start()
    for j in reversed(range(1, nf)):
        pl.semaphore_signal(
            barrier, inc=1, device_id={"freq": partner(mf, j, nf)}, device_id_type=MESH
        )
    peers = [partner(me, j, n) for j in range(n)]
    for j in reversed(range(1, n)):
        pl.semaphore_signal(barrier, inc=1, device_id={"facet": peers[j]}, device_id_type=MESH)
    for load in loads[4:]:
        load.start()
    loads[0].wait()
    flags = flg[...].astype(jnp.float32)
    place = kept_rows(flags).astype(jnp.int32)
    for load in loads[1:4]:
        load.wait()
    live = wts[...] * flags
    blocks, rows = flags.shape
    per_block = KEEP // LANES
    four = blocks * per_block
    slot_at = lax.broadcasted_iota(jnp.int32, (KEEP, rows), 0)
    for b in range(blocks):
        chosen = jnp.where(place[b:b + 1, :] == slot_at, 1.0, 0.0).astype(jnp.bfloat16)
        values = jnp.concatenate([vis[b] * live[b:b + 1, :], uv[b].astype(jnp.float32)], axis=0)
        packed = lax.dot_general(split3(values), chosen, NT, preferred_element_type=jnp.float32)
        packed = packed[0:4] + packed[4:8] + packed[8:12]
        for q in range(4):
            for h in range(per_block):
                row = (q % 2) * four + b * per_block + h
                buf[0, q // 2, row:row + 1, :] = packed[q:q + 1, h * LANES:(h + 1) * LANES]

    pl.semaphore_wait(barrier, n - 1 + nf - 1)
    sends = [
        pltpu.make_async_remote_copy(
            src_ref=buf.at[0],
            dst_ref=buf.at[j],
            send_sem=send_sem.at[j],
            recv_sem=recv_sem.at[j],
            device_id={"facet": peers[j]},
            device_id_type=MESH,
        )
        for j in range(1, n)
    ]
    for send in reversed(sends):
        send.start()

    for load in loads[4:]:
        load.wait()

    tall = 2 * four
    steps = plan.shape[1]
    row_at = lax.broadcasted_iota(jnp.int32, (tall, steps), 0)
    local = sum(
        jnp.where((row_at >= h * four + b * per_block) & (row_at < h * four + (b + 1) * per_block), b, 0)
        for h in range(2) for b in range(1, blocks)
    )
    read = plan[...] - local
    gain = beam[...] * scale
    gains = [
        jnp.sum(jnp.where(read == peers[j] * blocks, gain, 0.0), axis=1, keepdims=True)
        for j in range(n)
    ]

    high_row = lax.broadcasted_iota(jnp.int32, (tall, LANES), 0) < four
    first = facets[...] * P_SIZE - IMG // 2
    factor = jnp.where(high_row, 2 * first[:, 0:1] + (P_SIZE - 1), 2 * first[:, 1:2])
    sign = jnp.where(high_row, -1.0, 1.0)

    def swap(x):
        return jnp.concatenate([x[:, four:], x[:, :four]], axis=1)

    def tabulate(lo, hi):
        count = hi - lo
        cells = buf[lo:hi, 1]
        half = cos_sin(cells * (math.pi / IMG))
        turns = cells.astype(jnp.int32) * factor[None]
        turns = turns + swap(turns)
        turns = ((turns + IMG) & (2 * IMG - 1)) - IMG
        base = square(cos_sin(turns.astype(jnp.float32) * (math.pi / (2 * IMG))))
        x = buf[lo:hi, 0] * jnp.stack(
            [jnp.broadcast_to(gains[j], (tall, LANES)) for j in range(lo, hi)]
        )
        amp[lo:hi] = x * base[0] + swap(x) * (base[1] * sign[None])
        half_c[lo:hi] = half[0]
        half_s[lo:hi] = half[1]
        z = square(half)
        one = (jnp.ones_like(z[0]), jnp.zeros_like(z[0]))
        fine = powers(z, FINE)
        fine[0] = one
        step_c[lo:hi], step_s[lo:hi] = square(fine[FINE // 2])
        for ref, part in ((fine_c, 0), (fine_s, 1)):
            for k, entry in enumerate(fine):
                for i in range(count):
                    at = ((lo + i) * FINE + k) * tall
                    ref[at:at + tall, :] = entry[part][i]

    def image_terms(slot, sums):
        cu, su, re, im = [], [], [], []
        for r in range(four):
            def pick(row):
                at = pl.ds(slot * (FINE * tall) + row, FINE, stride=tall)
                return fine_c[at, :], fine_s[at, :]

            def line(refs, row):
                return refs[0][slot, row:row + 1, :], refs[1][slot, row:row + 1, :]

            def climb(start, row, rows_at):
                step = line((step_c, step_s), row)
                double = jnp.broadcast_to(step[0] + step[0], (FINE, LANES))
                table = [start, times(step, start)]
                while len(table) * FINE < rows_at:
                    table.append(
                        tuple(double * now - past for past, now in zip(table[-2], table[-1]))
                    )
                return table

            u = times(line((half_c, half_s), r), pick(r))
            v = times(
                (amp[slot, r:r + 1, :], amp[slot, four + r:four + r + 1, :]),
                pick(four + r),
            )
            left = climb(u, r, HALF)
            right = climb(v, four + r, P_SIZE)
            for kept, table, part in ((cu, left, 0), (su, left, 1), (re, right, 0), (im, right, 1)):
                kept.append(
                    jnp.concatenate([entry[part] for entry in table], axis=0).astype(jnp.bfloat16)
                )
        cu, su, re, im = (jnp.concatenate(kept, axis=1) for kept in (cu, su, re, im))
        return (
            sums[0] + lax.dot_general(cu, re, NT, preferred_element_type=jnp.float32),
            sums[1] + lax.dot_general(su, im, NT, preferred_element_type=jnp.float32),
        )

    sums = (jnp.zeros((HALF, P_SIZE), jnp.float32),) * 2
    for lo, hi in arrival_groups(n):
        for j in range(max(lo, 1), hi):
            sends[j - 1].wait_recv()
        tabulate(lo, hi)
        sums = lax.fori_loop(lo, hi, image_terms, sums, unroll=hi - lo if hi - lo <= 8 else 1)
    even, odd = sums

    share = P_SIZE // nf
    for f in range(nf):
        if f < nf // 2:
            at = (nf // 2 - 1 - f) * share
            stage[f] = even[at:at + share] + odd[at:at + share]
        else:
            at = (f - nf // 2) * share
            stage[f] = even[at:at + share] - odd[at:at + share]
    exchanges = []
    for j in reversed(range(1, nf)):
        to = partner(mf, j, nf)
        exchanges.append(
            pltpu.make_async_remote_copy(
                src_ref=stage.at[to],
                dst_ref=rbuf.at[j],
                send_sem=rsend_sem.at[j],
                recv_sem=rrecv_sem.at[j],
                device_id={"freq": to},
                device_id_type=MESH,
            )
        )
        exchanges[-1].start()
    total = stage[mf]
    for exchange in exchanges:
        exchange.wait_recv()
    for j in range(1, nf):
        total = total + rbuf[j]

    row8 = lax.broadcasted_iota(jnp.int32, (8, P_SIZE), 0)
    mirrored = []
    for k in reversed(range(share // 8)):
        y = pltpu.roll(total[k * 8:(k + 1) * 8], 4, 0)
        y = jnp.where((row8 & 2) != 0, pltpu.roll(y, 2, 0), pltpu.roll(y, 6, 0))
        y = jnp.where((row8 & 1) != 0, pltpu.roll(y, 1, 0), pltpu.roll(y, 7, 0))
        mirrored.append(y)
    mirrored = jnp.concatenate(mirrored, axis=0)
    out_ref[0] = jnp.where(mf < nf // 2, mirrored, total)
    for copy in sends + exchanges:
        copy.wait_send()


def body(n, nf, scale, visibilities, weights, uv_cells, flags, plan, beam, facets):
    blocks, _, rows = visibilities.shape
    four = blocks * (KEEP // LANES)
    tall = 2 * four
    share = P_SIZE // nf
    steps = plan.shape[0]
    f32, i32 = jnp.float32, jnp.int32
    return pl.pallas_call(
        functools.partial(kernel, n, nf, scale),
        out_shape=pltpu.VMEM((1, share, P_SIZE), f32),
        in_specs=[pl.BlockSpec(memory_space=pltpu.HBM)] * 7,
        out_specs=pl.BlockSpec(memory_space=pltpu.VMEM),
        scratch_shapes=[
            pltpu.VMEM((blocks, 2, rows), f32),
            pltpu.VMEM((blocks, rows), f32),
            pltpu.VMEM((blocks, 2, rows), i32),
            pltpu.VMEM((blocks, rows), i32),
            pltpu.VMEM((1, steps), i32),
            pltpu.VMEM((1, steps), f32),
            pltpu.VMEM((1, 2), i32),
            pltpu.VMEM((n, 2, tall, LANES), f32),
            pltpu.VMEM((n * FINE * tall, LANES), f32),
            pltpu.VMEM((n * FINE * tall, LANES), f32),
            pltpu.VMEM((n, tall, LANES), f32),
            pltpu.VMEM((n, tall, LANES), f32),
            pltpu.VMEM((n, tall, LANES), f32),
            pltpu.VMEM((n, tall, LANES), f32),
            pltpu.VMEM((n, tall, LANES), f32),
            pltpu.VMEM((nf, share, P_SIZE), f32),
            pltpu.VMEM((nf, share, P_SIZE), f32),
            pltpu.SemaphoreType.DMA((7,)),
            pltpu.SemaphoreType.DMA((n,)),
            pltpu.SemaphoreType.DMA((n,)),
            pltpu.SemaphoreType.DMA((nf,)),
            pltpu.SemaphoreType.DMA((nf,)),
        ],
        compiler_params=pltpu.CompilerParams(
            collective_id=0, has_side_effects=True, vmem_limit_bytes=62 * 1024 * 1024
        ),
        name="facet_image",
    )(visibilities, weights, uv_cells, flags, plan.reshape(1, steps), beam, facets)


def solution(mesh):
    n, nf = mesh.shape["facet"], mesh.shape["freq"]
    in_specs = (
        P("facet", None, "freq"),
        P("facet", "freq"),
        P("facet", None, "freq"),
        P("facet", "freq"),
        P(),
        P("facet", None),
        P("facet", None),
    )
    out_specs = P("facet", "freq", None)

    def whole(visibilities, *others):
        scale = 2.0 / math.sqrt(visibilities.shape[0] * visibilities.shape[2])
        return jax.shard_map(
            functools.partial(body, n, nf, scale),
            mesh=mesh, in_specs=in_specs, out_specs=out_specs, check_vma=False,
        )(visibilities, *others)

    return whole
```

```python
import functools
import math

import jax
import jax.numpy as jnp
from jax import lax
from jax.experimental import pallas as pl
from jax.experimental.pallas import tpu as pltpu
from jax.sharding import PartitionSpec as P

P_SIZE = 128
IMG = 32768
KEEP = 256
LANES = 128
HALF = P_SIZE // 2
FINE = 8
MESH = pl.DeviceIdType.MESH
NT = (((1,), (1,)), ((), ()))


def cos_sin(x):
    q = x * x
    s = jnp.full_like(q, -1.0 / math.factorial(11))
    for order in (9, 7, 5, 3, 1):
        s = s * q + (-1.0) ** (order // 2) / math.factorial(order)
    c = jnp.full_like(q, 1.0 / math.factorial(12))
    for order in (10, 8, 6, 4, 2, 0):
        c = c * q + (-1.0) ** (order // 2) / math.factorial(order)
    return c, s * x


def times(a, b):
    return a[0] * b[0] - a[1] * b[1], a[0] * b[1] + a[1] * b[0]


def square(a):
    return a[0] * a[0] - a[1] * a[1], 2.0 * (a[0] * a[1])


def powers(z, count):
    found = [None, z]
    for k in range(2, count):
        half = found[k // 2]
        found.append(square(half) if k % 2 == 0 else times(found[k // 2 + 1], half))
    return found


def partner(me, j, n):
    assert n & (n - 1) == 0
    found, bit = 0, 1
    while bit < n:
        own = lax.rem(me // bit, 2)
        found = found + bit * (1 - own if j & bit else own)
        bit *= 2
    return found


def arrival_groups(n):
    return [(0, 1), (1, n // 2), (n // 2, n - n // 4), (n - n // 4, n)]


def kept_rows(flags):
    blocks, rows = flags.shape
    pieces = [flags[:, j * LANES:(j + 1) * LANES] for j in range(rows // LANES)]
    stacked = jnp.concatenate(pieces, axis=0)
    lower = lax.broadcasted_iota(jnp.int32, (LANES, LANES), 1) <= lax.broadcasted_iota(
        jnp.int32, (LANES, LANES), 0
    )
    inside = lax.dot_general(
        stacked.astype(jnp.bfloat16),
        jnp.where(lower, 1.0, 0.0).astype(jnp.bfloat16),
        NT,
        preferred_element_type=jnp.float32,
    )
    totals = jnp.sum(stacked, axis=1, keepdims=True)
    before = jnp.zeros((blocks, 1), jnp.float32)
    places = []
    for j, piece in enumerate(pieces):
        own = slice(j * blocks, (j + 1) * blocks)
        places.append(jnp.where(piece > 0.5, inside[own] + before - 1.0, -1.0))
        before = before + totals[own]
    return jnp.concatenate(places, axis=1)


def split3(x):
    high = x.astype(jnp.bfloat16).astype(jnp.float32)
    rest = x - high
    middle = rest.astype(jnp.bfloat16).astype(jnp.float32)
    low = rest - middle
    return jnp.concatenate([high, middle, low, jnp.zeros_like(x)], axis=0).astype(jnp.bfloat16)


def kernel(
    n, nf, scale,
    vis_hbm, w_hbm, uv_hbm, flags_hbm, plan_hbm, beam_hbm, facets_hbm,
    out_ref,
    vis, wts, uv, flg, plan, beam, facets,
    buf, fine_c, fine_s, step_c, step_s, half_c, half_s, amp, stage, rbuf,
    in_sem, send_sem, recv_sem, rsend_sem, rrecv_sem,
):
    mf = lax.axis_index("freq")
    me = lax.axis_index("facet")
    barrier = pltpu.get_barrier_semaphore()
    loads = [
        pltpu.make_async_copy(src, dst, in_sem.at[k])
        for k, (src, dst) in enumerate(
            [(flags_hbm, flg), (vis_hbm, vis), (w_hbm, wts), (uv_hbm, uv),
             (plan_hbm, plan), (beam_hbm, beam), (facets_hbm, facets)]
        )
    ]
    for load in loads[:4]:
        load.start()
    for j in reversed(range(1, nf)):
        pl.semaphore_signal(
            barrier, inc=1, device_id={"freq": partner(mf, j, nf)}, device_id_type=MESH
        )
    peers = [partner(me, j, n) for j in range(n)]
    for j in reversed(range(1, n)):
        pl.semaphore_signal(barrier, inc=1, device_id={"facet": peers[j]}, device_id_type=MESH)
    for load in loads[4:]:
        load.start()
    loads[0].wait()
    flags = flg[...].astype(jnp.float32)
    place = kept_rows(flags).astype(jnp.int32)
    for load in loads[1:4]:
        load.wait()
    live = wts[...] * flags
    blocks, rows = flags.shape
    per_block = KEEP // LANES
    four = blocks * per_block
    slot_at = lax.broadcasted_iota(jnp.int32, (KEEP, rows), 0)
    for b in range(blocks):
        chosen = jnp.where(place[b:b + 1, :] == slot_at, 1.0, 0.0).astype(jnp.bfloat16)
        values = jnp.concatenate([vis[b] * live[b:b + 1, :], uv[b].astype(jnp.float32)], axis=0)
        packed = lax.dot_general(split3(values), chosen, NT, preferred_element_type=jnp.float32)
        packed = packed[0:4] + packed[4:8] + packed[8:12]
        for q in range(4):
            for h in range(per_block):
                row = (q % 2) * four + b * per_block + h
                buf[0, q // 2, row:row + 1, :] = packed[q:q + 1, h * LANES:(h + 1) * LANES]

    pl.semaphore_wait(barrier, n - 1 + nf - 1)
    sends = [
        pltpu.make_async_remote_copy(
            src_ref=buf.at[0],
            dst_ref=buf.at[j],
            send_sem=send_sem.at[j],
            recv_sem=recv_sem.at[j],
            device_id={"facet": peers[j]},
            device_id_type=MESH,
        )
        for j in range(1, n)
    ]
    for send in reversed(sends):
        send.start()

    for load in loads[4:]:
        load.wait()

    tall = 2 * four
    steps = plan.shape[1]
    row_at = lax.broadcasted_iota(jnp.int32, (tall, steps), 0)
    local = sum(
        jnp.where((row_at >= h * four + b * per_block) & (row_at < h * four + (b + 1) * per_block), b, 0)
        for h in range(2) for b in range(1, blocks)
    )
    read = plan[...] - local
    gain = beam[...] * scale
    gains = [
        jnp.sum(jnp.where(read == peers[j] * blocks, gain, 0.0), axis=1, keepdims=True)
        for j in range(n)
    ]

    high_row = lax.broadcasted_iota(jnp.int32, (tall, LANES), 0) < four
    first = facets[...] * P_SIZE - IMG // 2
    factor = jnp.where(high_row, 2 * first[:, 0:1] + (P_SIZE - 1), 2 * first[:, 1:2])
    sign = jnp.where(high_row, -1.0, 1.0)

    def swap(x):
        return jnp.concatenate([x[:, four:], x[:, :four]], axis=1)

    def tabulate(lo, hi):
        count = hi - lo
        cells = buf[lo:hi, 1]
        half = cos_sin(cells * (math.pi / IMG))
        turns = cells.astype(jnp.int32) * factor[None]
        turns = turns + swap(turns)
        turns = ((turns + IMG) & (2 * IMG - 1)) - IMG
        base = square(cos_sin(turns.astype(jnp.float32) * (math.pi / (2 * IMG))))
        x = buf[lo:hi, 0] * jnp.stack(
            [jnp.broadcast_to(gains[j], (tall, LANES)) for j in range(lo, hi)]
        )
        amp[lo:hi] = x * base[0] + swap(x) * (base[1] * sign[None])
        half_c[lo:hi] = half[0]
        half_s[lo:hi] = half[1]
        z = square(half)
        one = (jnp.ones_like(z[0]), jnp.zeros_like(z[0]))
        fine = powers(z, FINE)
        fine[0] = one
        step_c[lo:hi], step_s[lo:hi] = square(fine[FINE // 2])
        for ref, part in ((fine_c, 0), (fine_s, 1)):
            for k, entry in enumerate(fine):
                for i in range(count):
                    at = ((lo + i) * FINE + k) * tall
                    ref[at:at + tall, :] = entry[part][i]

    def image_terms(slot, sums):
        cu, su, re, im = [], [], [], []
        for r in range(four):
            def pick(row):
                at = pl.ds(slot * (FINE * tall) + row, FINE, stride=tall)
                return fine_c[at, :], fine_s[at, :]

            def line(refs, row):
                return refs[0][slot, row:row + 1, :], refs[1][slot, row:row + 1, :]

            def climb(start, row, rows_at):
                step = line((step_c, step_s), row)
                double = jnp.broadcast_to(step[0] + step[0], (FINE, LANES))
                table = [start, times(step, start)]
                while len(table) * FINE < rows_at:
                    table.append(
                        tuple(double * now - past for past, now in zip(table[-2], table[-1]))
                    )
                return table

            u = times(line((half_c, half_s), r), pick(r))
            v = times(
                (amp[slot, r:r + 1, :], amp[slot, four + r:four + r + 1, :]),
                pick(four + r),
            )
            left = climb(u, r, HALF)
            right = climb(v, four + r, P_SIZE)
            for kept, table, part in ((cu, left, 0), (su, left, 1), (re, right, 0), (im, right, 1)):
                kept.append(
                    jnp.concatenate([entry[part] for entry in table], axis=0).astype(jnp.bfloat16)
                )
        left = jnp.concatenate([jnp.concatenate(kept, axis=1) for kept in (cu, su)], axis=0)
        right = jnp.concatenate([jnp.concatenate(kept, axis=1) for kept in (re, im)], axis=0)
        term = lax.dot_general(left, right, NT, preferred_element_type=jnp.float32)
        return sums[0] + term[:HALF, :P_SIZE], sums[1] + term[HALF:, P_SIZE:]

    sums = (jnp.zeros((HALF, P_SIZE), jnp.float32),) * 2
    for lo, hi in arrival_groups(n):
        for j in range(max(lo, 1), hi):
            sends[j - 1].wait_recv()
        tabulate(lo, hi)
        sums = lax.fori_loop(lo, hi, image_terms, sums, unroll=hi - lo if hi - lo <= 8 else 1)
    even, odd = sums

    share = P_SIZE // nf
    for f in range(nf):
        if f < nf // 2:
            at = (nf // 2 - 1 - f) * share
            stage[f] = even[at:at + share] + odd[at:at + share]
        else:
            at = (f - nf // 2) * share
            stage[f] = even[at:at + share] - odd[at:at + share]
    exchanges = []
    for j in reversed(range(1, nf)):
        to = partner(mf, j, nf)
        exchanges.append(
            pltpu.make_async_remote_copy(
                src_ref=stage.at[to],
                dst_ref=rbuf.at[j],
                send_sem=rsend_sem.at[j],
                recv_sem=rrecv_sem.at[j],
                device_id={"freq": to},
                device_id_type=MESH,
            )
        )
        exchanges[-1].start()
    total = stage[mf]
    for exchange in exchanges:
        exchange.wait_recv()
    for j in range(1, nf):
        total = total + rbuf[j]

    row8 = lax.broadcasted_iota(jnp.int32, (8, P_SIZE), 0)
    mirrored = []
    for k in reversed(range(share // 8)):
        y = pltpu.roll(total[k * 8:(k + 1) * 8], 4, 0)
        y = jnp.where((row8 & 2) != 0, pltpu.roll(y, 2, 0), pltpu.roll(y, 6, 0))
        y = jnp.where((row8 & 1) != 0, pltpu.roll(y, 1, 0), pltpu.roll(y, 7, 0))
        mirrored.append(y)
    mirrored = jnp.concatenate(mirrored, axis=0)
    out_ref[0] = jnp.where(mf < nf // 2, mirrored, total)
    for copy in sends + exchanges:
        copy.wait_send()


def body(n, nf, scale, visibilities, weights, uv_cells, flags, plan, beam, facets):
    blocks, _, rows = visibilities.shape
    four = blocks * (KEEP // LANES)
    tall = 2 * four
    share = P_SIZE // nf
    steps = plan.shape[0]
    f32, i32 = jnp.float32, jnp.int32
    return pl.pallas_call(
        functools.partial(kernel, n, nf, scale),
        out_shape=pltpu.VMEM((1, share, P_SIZE), f32),
        in_specs=[pl.BlockSpec(memory_space=pltpu.HBM)] * 7,
        out_specs=pl.BlockSpec(memory_space=pltpu.VMEM),
        scratch_shapes=[
            pltpu.VMEM((blocks, 2, rows), f32),
            pltpu.VMEM((blocks, rows), f32),
            pltpu.VMEM((blocks, 2, rows), i32),
            pltpu.VMEM((blocks, rows), i32),
            pltpu.VMEM((1, steps), i32),
            pltpu.VMEM((1, steps), f32),
            pltpu.VMEM((1, 2), i32),
            pltpu.VMEM((n, 2, tall, LANES), f32),
            pltpu.VMEM((n * FINE * tall, LANES), f32),
            pltpu.VMEM((n * FINE * tall, LANES), f32),
            pltpu.VMEM((n, tall, LANES), f32),
            pltpu.VMEM((n, tall, LANES), f32),
            pltpu.VMEM((n, tall, LANES), f32),
            pltpu.VMEM((n, tall, LANES), f32),
            pltpu.VMEM((n, tall, LANES), f32),
            pltpu.VMEM((nf, share, P_SIZE), f32),
            pltpu.VMEM((nf, share, P_SIZE), f32),
            pltpu.SemaphoreType.DMA((7,)),
            pltpu.SemaphoreType.DMA((n,)),
            pltpu.SemaphoreType.DMA((n,)),
            pltpu.SemaphoreType.DMA((nf,)),
            pltpu.SemaphoreType.DMA((nf,)),
        ],
        compiler_params=pltpu.CompilerParams(
            collective_id=0, has_side_effects=True, vmem_limit_bytes=62 * 1024 * 1024
        ),
        name="facet_image",
    )(visibilities, weights, uv_cells, flags, plan.reshape(1, steps), beam, facets)


def solution(mesh):
    n, nf = mesh.shape["facet"], mesh.shape["freq"]
    in_specs = (
        P("facet", None, "freq"),
        P("facet", "freq"),
        P("facet", None, "freq"),
        P("facet", "freq"),
        P(),
        P("facet", None),
        P("facet", None),
    )
    out_specs = P("facet", "freq", None)

    def whole(visibilities, *others):
        scale = 2.0 / math.sqrt(visibilities.shape[0] * visibilities.shape[2])
        return jax.shard_map(
            functools.partial(body, n, nf, scale),
            mesh=mesh, in_specs=in_specs, out_specs=out_specs, check_vma=False,
        )(visibilities, *others)

    return whole
```

```python
import functools
import math

import jax
import jax.numpy as jnp
from jax import lax
from jax.experimental import pallas as pl
from jax.experimental.pallas import tpu as pltpu
from jax.sharding import PartitionSpec as P

P_SIZE = 128
IMG = 32768
KEEP = 256
LANES = 128
HALF = P_SIZE // 2
FINE = 8
MESH = pl.DeviceIdType.MESH
NT = (((1,), (1,)), ((), ()))


def cos_sin(x):
    q = x * x
    q2 = q * q
    q4 = q2 * q2

    def pairwise(first):
        terms = [(-1.0) ** (k // 2) / math.factorial(k) for k in range(first, 14, 2)]
        low = (terms[0] + terms[1] * q) + (terms[2] + terms[3] * q) * q2
        high = terms[4] + terms[5] * q
        if len(terms) > 6:
            high = high + terms[6] * q2
        return low + high * q4

    c, s = pairwise(0), pairwise(1)
    return c, s * x


def times(a, b):
    return a[0] * b[0] - a[1] * b[1], a[0] * b[1] + a[1] * b[0]


def square(a):
    return a[0] * a[0] - a[1] * a[1], 2.0 * (a[0] * a[1])


def powers(z, count):
    found = [None, z]
    for k in range(2, count):
        half = found[k // 2]
        found.append(square(half) if k % 2 == 0 else times(found[k // 2 + 1], half))
    return found


def partner(me, j, n):
    assert n & (n - 1) == 0
    found, bit = 0, 1
    while bit < n:
        own = lax.rem(me // bit, 2)
        found = found + bit * (1 - own if j & bit else own)
        bit *= 2
    return found


def arrival_groups(n):
    return [(0, 1), (1, n // 2), (n // 2, n - n // 4), (n - n // 4, n - 1), (n - 1, n)]


def kept_rows(flags):
    blocks, rows = flags.shape
    pieces = [flags[:, j * LANES:(j + 1) * LANES] for j in range(rows // LANES)]
    stacked = jnp.concatenate(pieces, axis=0)
    lower = lax.broadcasted_iota(jnp.int32, (LANES, LANES), 1) <= lax.broadcasted_iota(
        jnp.int32, (LANES, LANES), 0
    )
    inside = lax.dot_general(
        stacked.astype(jnp.bfloat16),
        jnp.where(lower, 1.0, 0.0).astype(jnp.bfloat16),
        NT,
        preferred_element_type=jnp.float32,
    )
    totals = jnp.sum(stacked, axis=1, keepdims=True)
    before = jnp.zeros((blocks, 1), jnp.float32)
    places = []
    for j, piece in enumerate(pieces):
        own = slice(j * blocks, (j + 1) * blocks)
        places.append(jnp.where(piece > 0.5, inside[own] + before - 1.0, -1.0))
        before = before + totals[own]
    return jnp.concatenate(places, axis=1)


def split3(x):
    high = x.astype(jnp.bfloat16).astype(jnp.float32)
    rest = x - high
    middle = rest.astype(jnp.bfloat16).astype(jnp.float32)
    low = rest - middle
    return jnp.concatenate([high, middle, low, jnp.zeros_like(x)], axis=0).astype(jnp.bfloat16)


def kernel(
    n, nf, scale,
    vis_hbm, w_hbm, uv_hbm, flags_hbm, plan_hbm, beam_hbm, facets_hbm,
    out_ref,
    vis, wts, uv, flg, plan, beam, facets,
    buf, fine_c, fine_s, step_c, step_s, half_c, half_s, amp, stage, rbuf,
    in_sem, send_sem, recv_sem, rsend_sem, rrecv_sem,
):
    mf = lax.axis_index("freq")
    me = lax.axis_index("facet")
    barrier = pltpu.get_barrier_semaphore()
    loads = [
        pltpu.make_async_copy(src, dst, in_sem.at[k])
        for k, (src, dst) in enumerate(
            [(flags_hbm, flg), (vis_hbm, vis), (w_hbm, wts), (uv_hbm, uv),
             (plan_hbm, plan), (beam_hbm, beam), (facets_hbm, facets)]
        )
    ]
    for load in loads[:4]:
        load.start()
    for j in reversed(range(1, nf)):
        pl.semaphore_signal(
            barrier, inc=1, device_id={"freq": partner(mf, j, nf)}, device_id_type=MESH
        )
    peers = [partner(me, j, n) for j in range(n)]
    for j in reversed(range(1, n)):
        pl.semaphore_signal(barrier, inc=1, device_id={"facet": peers[j]}, device_id_type=MESH)
    for load in loads[4:]:
        load.start()
    loads[0].wait()
    flags = flg[...].astype(jnp.float32)
    place = kept_rows(flags).astype(jnp.int32)
    for load in loads[1:4]:
        load.wait()
    live = wts[...] * flags
    blocks, rows = flags.shape
    per_block = KEEP // LANES
    four = blocks * per_block
    slot_at = lax.broadcasted_iota(jnp.int32, (KEEP, rows), 0)
    for b in range(blocks):
        chosen = jnp.where(place[b:b + 1, :] == slot_at, 1.0, 0.0).astype(jnp.bfloat16)
        values = jnp.concatenate([vis[b] * live[b:b + 1, :], uv[b].astype(jnp.float32)], axis=0)
        packed = lax.dot_general(split3(values), chosen, NT, preferred_element_type=jnp.float32)
        packed = packed[0:4] + packed[4:8] + packed[8:12]
        for q in range(4):
            for h in range(per_block):
                row = (q % 2) * four + b * per_block + h
                buf[0, q // 2, row:row + 1, :] = packed[q:q + 1, h * LANES:(h + 1) * LANES]

    pl.semaphore_wait(barrier, n - 1 + nf - 1)
    sends = [
        pltpu.make_async_remote_copy(
            src_ref=buf.at[0],
            dst_ref=buf.at[j],
            send_sem=send_sem.at[j],
            recv_sem=recv_sem.at[j],
            device_id={"facet": peers[j]},
            device_id_type=MESH,
        )
        for j in range(1, n)
    ]
    for send in reversed(sends):
        send.start()

    for load in loads[4:]:
        load.wait()

    tall = 2 * four
    steps = plan.shape[1]
    row_at = lax.broadcasted_iota(jnp.int32, (tall, steps), 0)
    local = sum(
        jnp.where((row_at >= h * four + b * per_block) & (row_at < h * four + (b + 1) * per_block), b, 0)
        for h in range(2) for b in range(1, blocks)
    )
    read = plan[...] - local
    gain = beam[...] * scale
    gains = [
        jnp.sum(jnp.where(read == peers[j] * blocks, gain, 0.0), axis=1, keepdims=True)
        for j in range(n)
    ]

    high_row = lax.broadcasted_iota(jnp.int32, (tall, LANES), 0) < four
    first = facets[...] * P_SIZE - IMG // 2
    factor = jnp.where(high_row, 2 * first[:, 0:1] + (P_SIZE - 1), 2 * first[:, 1:2])
    sign = jnp.where(high_row, -1.0, 1.0)

    def swap(x):
        return jnp.concatenate([x[:, four:], x[:, :four]], axis=1)

    def tabulate(lo, hi):
        count = hi - lo
        cells = buf[lo:hi, 1]
        half = cos_sin(cells * (math.pi / IMG))
        turns = cells.astype(jnp.int32) * factor[None]
        turns = turns + swap(turns)
        turns = ((turns + IMG) & (2 * IMG - 1)) - IMG
        base = square(cos_sin(turns.astype(jnp.float32) * (math.pi / (2 * IMG))))
        x = buf[lo:hi, 0] * jnp.stack(
            [jnp.broadcast_to(gains[j], (tall, LANES)) for j in range(lo, hi)]
        )
        amp[lo:hi] = x * base[0] + swap(x) * (base[1] * sign[None])
        half_c[lo:hi] = half[0]
        half_s[lo:hi] = half[1]
        z = square(half)
        one = (jnp.ones_like(z[0]), jnp.zeros_like(z[0]))
        fine = powers(z, FINE)
        fine[0] = one
        step_c[lo:hi], step_s[lo:hi] = square(fine[FINE // 2])
        for ref, part in ((fine_c, 0), (fine_s, 1)):
            for k, entry in enumerate(fine):
                for i in range(count):
                    at = ((lo + i) * FINE + k) * tall
                    ref[at:at + tall, :] = entry[part][i]

    def image_terms(slot, sums):
        cu, su, re, im = [], [], [], []
        for r in range(four):
            def pick(row):
                at = pl.ds(slot * (FINE * tall) + row, FINE, stride=tall)
                return fine_c[at, :], fine_s[at, :]

            def line(refs, row):
                return refs[0][slot, row:row + 1, :], refs[1][slot, row:row + 1, :]

            def climb(start, row, rows_at):
                step = line((step_c, step_s), row)
                double = jnp.broadcast_to(step[0] + step[0], (FINE, LANES))
                table = [start, times(step, start)]
                while len(table) * FINE < rows_at:
                    table.append(
                        tuple(double * now - past for past, now in zip(table[-2], table[-1]))
                    )
                return table

            u = times(line((half_c, half_s), r), pick(r))
            v = times(
                (amp[slot, r:r + 1, :], amp[slot, four + r:four + r + 1, :]),
                pick(four + r),
            )
            left = climb(u, r, HALF)
            right = climb(v, four + r, P_SIZE)
            for kept, table, part in ((cu, left, 0), (su, left, 1), (re, right, 0), (im, right, 1)):
                kept.append(
                    jnp.concatenate([entry[part] for entry in table], axis=0).astype(jnp.bfloat16)
                )
        cu, su, re, im = (jnp.concatenate(kept, axis=1) for kept in (cu, su, re, im))
        return (
            sums[0] + lax.dot_general(cu, re, NT, preferred_element_type=jnp.float32),
            sums[1] + lax.dot_general(su, im, NT, preferred_element_type=jnp.float32),
        )

    sums = (jnp.zeros((HALF, P_SIZE), jnp.float32),) * 2
    for lo, hi in arrival_groups(n):
        for j in range(max(lo, 1), hi):
            sends[j - 1].wait_recv()
        tabulate(lo, hi)
        sums = lax.fori_loop(lo, hi, image_terms, sums, unroll=hi - lo if hi - lo <= 8 else 1)
    even, odd = sums

    share = P_SIZE // nf
    for f in range(nf):
        if f < nf // 2:
            at = (nf // 2 - 1 - f) * share
            stage[f] = even[at:at + share] + odd[at:at + share]
        else:
            at = (f - nf // 2) * share
            stage[f] = even[at:at + share] - odd[at:at + share]
    exchanges = []
    for j in reversed(range(1, nf)):
        to = partner(mf, j, nf)
        exchanges.append(
            pltpu.make_async_remote_copy(
                src_ref=stage.at[to],
                dst_ref=rbuf.at[j],
                send_sem=rsend_sem.at[j],
                recv_sem=rrecv_sem.at[j],
                device_id={"freq": to},
                device_id_type=MESH,
            )
        )
        exchanges[-1].start()
    total = stage[mf]
    for exchange in exchanges:
        exchange.wait_recv()
    for j in range(1, nf):
        total = total + rbuf[j]

    row8 = lax.broadcasted_iota(jnp.int32, (8, P_SIZE), 0)
    mirrored = []
    for k in reversed(range(share // 8)):
        y = pltpu.roll(total[k * 8:(k + 1) * 8], 4, 0)
        y = jnp.where((row8 & 2) != 0, pltpu.roll(y, 2, 0), pltpu.roll(y, 6, 0))
        y = jnp.where((row8 & 1) != 0, pltpu.roll(y, 1, 0), pltpu.roll(y, 7, 0))
        mirrored.append(y)
    mirrored = jnp.concatenate(mirrored, axis=0)
    out_ref[0] = jnp.where(mf < nf // 2, mirrored, total)
    for copy in sends + exchanges:
        copy.wait_send()


def body(n, nf, scale, visibilities, weights, uv_cells, flags, plan, beam, facets):
    blocks, _, rows = visibilities.shape
    four = blocks * (KEEP // LANES)
    tall = 2 * four
    share = P_SIZE // nf
    steps = plan.shape[0]
    f32, i32 = jnp.float32, jnp.int32
    return pl.pallas_call(
        functools.partial(kernel, n, nf, scale),
        out_shape=pltpu.VMEM((1, share, P_SIZE), f32),
        in_specs=[pl.BlockSpec(memory_space=pltpu.HBM)] * 7,
        out_specs=pl.BlockSpec(memory_space=pltpu.VMEM),
        scratch_shapes=[
            pltpu.VMEM((blocks, 2, rows), f32),
            pltpu.VMEM((blocks, rows), f32),
            pltpu.VMEM((blocks, 2, rows), i32),
            pltpu.VMEM((blocks, rows), i32),
            pltpu.VMEM((1, steps), i32),
            pltpu.VMEM((1, steps), f32),
            pltpu.VMEM((1, 2), i32),
            pltpu.VMEM((n, 2, tall, LANES), f32),
            pltpu.VMEM((n * FINE * tall, LANES), f32),
            pltpu.VMEM((n * FINE * tall, LANES), f32),
            pltpu.VMEM((n, tall, LANES), f32),
            pltpu.VMEM((n, tall, LANES), f32),
            pltpu.VMEM((n, tall, LANES), f32),
            pltpu.VMEM((n, tall, LANES), f32),
            pltpu.VMEM((n, tall, LANES), f32),
            pltpu.VMEM((nf, share, P_SIZE), f32),
            pltpu.VMEM((nf, share, P_SIZE), f32),
            pltpu.SemaphoreType.DMA((7,)),
            pltpu.SemaphoreType.DMA((n,)),
            pltpu.SemaphoreType.DMA((n,)),
            pltpu.SemaphoreType.DMA((nf,)),
            pltpu.SemaphoreType.DMA((nf,)),
        ],
        compiler_params=pltpu.CompilerParams(
            collective_id=0, has_side_effects=True, vmem_limit_bytes=62 * 1024 * 1024
        ),
        name="facet_image",
    )(visibilities, weights, uv_cells, flags, plan.reshape(1, steps), beam, facets)


def solution(mesh):
    n, nf = mesh.shape["facet"], mesh.shape["freq"]
    in_specs = (
        P("facet", None, "freq"),
        P("facet", "freq"),
        P("facet", None, "freq"),
        P("facet", "freq"),
        P(),
        P("facet", None),
        P("facet", None),
    )
    out_specs = P("facet", "freq", None)

    def whole(visibilities, *others):
        scale = 2.0 / math.sqrt(visibilities.shape[0] * visibilities.shape[2])
        return jax.shard_map(
            functools.partial(body, n, nf, scale),
            mesh=mesh, in_specs=in_specs, out_specs=out_specs, check_vma=False,
        )(visibilities, *others)

    return whole
```

```python
import functools
import math

import jax
import jax.numpy as jnp
from jax import lax
from jax.experimental import pallas as pl
from jax.experimental.pallas import tpu as pltpu
from jax.sharding import PartitionSpec as P

P_SIZE = 128
IMG = 32768
KEEP = 256
LANES = 128
HALF = P_SIZE // 2
FINE = 8
MESH = pl.DeviceIdType.MESH
NT = (((1,), (1,)), ((), ()))


def cos_sin(x):
    q = x * x
    s = jnp.full_like(q, -1.0 / math.factorial(11))
    for order in (9, 7, 5, 3, 1):
        s = s * q + (-1.0) ** (order // 2) / math.factorial(order)
    c = jnp.full_like(q, 1.0 / math.factorial(12))
    for order in (10, 8, 6, 4, 2, 0):
        c = c * q + (-1.0) ** (order // 2) / math.factorial(order)
    return c, s * x


def times(a, b):
    return a[0] * b[0] - a[1] * b[1], a[0] * b[1] + a[1] * b[0]


def square(a):
    return a[0] * a[0] - a[1] * a[1], 2.0 * (a[0] * a[1])


def powers(z, count):
    found = [None, z]
    for k in range(2, count):
        half = found[k // 2]
        found.append(square(half) if k % 2 == 0 else times(found[k // 2 + 1], half))
    return found


def exclusive(a, b, n):
    found, bit = 0, 1
    while bit < n:
        found = found + bit * lax.rem(a // bit + b // bit, 2)
        bit *= 2
    return found


def partner(me, j, n):
    assert n & (n - 1) == 0
    found, bit = 0, 1
    while bit < n:
        own = lax.rem(me // bit, 2)
        found = found + bit * (1 - own if j & bit else own)
        bit *= 2
    return found


def arrival_groups(n):
    return [(0, 1), (1, n // 2), (n // 2, n - n // 4), (n - n // 4, n)]


def kept_rows(flags):
    blocks, rows = flags.shape
    pieces = [flags[:, j * LANES:(j + 1) * LANES] for j in range(rows // LANES)]
    stacked = jnp.concatenate(pieces, axis=0)
    lower = lax.broadcasted_iota(jnp.int32, (LANES, LANES), 1) <= lax.broadcasted_iota(
        jnp.int32, (LANES, LANES), 0
    )
    inside = lax.dot_general(
        stacked.astype(jnp.bfloat16),
        jnp.where(lower, 1.0, 0.0).astype(jnp.bfloat16),
        NT,
        preferred_element_type=jnp.float32,
    )
    totals = jnp.sum(stacked, axis=1, keepdims=True)
    before = jnp.zeros((blocks, 1), jnp.float32)
    places = []
    for j, piece in enumerate(pieces):
        own = slice(j * blocks, (j + 1) * blocks)
        places.append(jnp.where(piece > 0.5, inside[own] + before - 1.0, -1.0))
        before = before + totals[own]
    return jnp.concatenate(places, axis=1)


def split3(x):
    high = x.astype(jnp.bfloat16).astype(jnp.float32)
    rest = x - high
    middle = rest.astype(jnp.bfloat16).astype(jnp.float32)
    low = rest - middle
    return jnp.concatenate([high, middle, low, jnp.zeros_like(x)], axis=0).astype(jnp.bfloat16)


def kernel(
    n, nf, scale,
    vis_hbm, w_hbm, uv_hbm, flags_hbm, plan_hbm, beam_hbm, facets_hbm,
    out_ref,
    vis, wts, uv, flg, plan, beam, facets,
    buf, fine_c, fine_s, step_c, step_s, half_c, half_s, amp, stage, rbuf,
    in_sem, send_sem, recv_sem, rsend_sem, rrecv_sem,
):
    mf = lax.axis_index("freq")
    me = lax.axis_index("facet")
    barrier = pltpu.get_barrier_semaphore()
    loads = [
        pltpu.make_async_copy(src, dst, in_sem.at[k])
        for k, (src, dst) in enumerate(
            [(flags_hbm, flg), (vis_hbm, vis), (w_hbm, wts), (uv_hbm, uv),
             (plan_hbm, plan), (beam_hbm, beam), (facets_hbm, facets)]
        )
    ]
    for load in loads[:4]:
        load.start()
    for j in reversed(range(1, nf)):
        pl.semaphore_signal(
            barrier, inc=1, device_id={"freq": partner(mf, j, nf)}, device_id_type=MESH
        )
    peers = [partner(me, j, n) for j in range(n)]
    for j in reversed(range(1, n)):
        pl.semaphore_signal(barrier, inc=1, device_id={"facet": peers[j]}, device_id_type=MESH)
    for load in loads[4:]:
        load.start()
    loads[0].wait()
    flags = flg[...].astype(jnp.float32)
    place = kept_rows(flags).astype(jnp.int32)
    for load in loads[1:4]:
        load.wait()
    live = wts[...] * flags
    blocks, rows = flags.shape
    per_block = KEEP // LANES
    four = blocks * per_block
    slot_at = lax.broadcasted_iota(jnp.int32, (KEEP, rows), 0)
    for b in range(blocks):
        chosen = jnp.where(place[b:b + 1, :] == slot_at, 1.0, 0.0).astype(jnp.bfloat16)
        values = jnp.concatenate([vis[b] * live[b:b + 1, :], uv[b].astype(jnp.float32)], axis=0)
        packed = lax.dot_general(split3(values), chosen, NT, preferred_element_type=jnp.float32)
        packed = packed[0:4] + packed[4:8] + packed[8:12]
        for q in range(4):
            for h in range(per_block):
                row = (q % 2) * four + b * per_block + h
                buf[0, q // 2, row:row + 1, :] = packed[q:q + 1, h * LANES:(h + 1) * LANES]

    pl.semaphore_wait(barrier, n - 1 + nf - 1)
    def to_peer(slot, device, k):
        return pltpu.make_async_remote_copy(
            src_ref=buf.at[0],
            dst_ref=buf.at[slot],
            send_sem=send_sem.at[k],
            recv_sem=recv_sem.at[slot],
            device_id={"facet": device},
            device_id_type=MESH,
        )

    sends = []
    for k in range(n - 1):
        device = k + jnp.where(me <= k, 1, 0)
        sends.append(to_peer(exclusive(me, device, n), device, k))
        sends[-1].start()

    for load in loads[4:]:
        load.wait()

    tall = 2 * four
    steps = plan.shape[1]
    row_at = lax.broadcasted_iota(jnp.int32, (tall, steps), 0)
    local = sum(
        jnp.where((row_at >= h * four + b * per_block) & (row_at < h * four + (b + 1) * per_block), b, 0)
        for h in range(2) for b in range(1, blocks)
    )
    read = plan[...] - local
    gain = beam[...] * scale
    gains = [
        jnp.sum(jnp.where(read == peers[j] * blocks, gain, 0.0), axis=1, keepdims=True)
        for j in range(n)
    ]

    high_row = lax.broadcasted_iota(jnp.int32, (tall, LANES), 0) < four
    first = facets[...] * P_SIZE - IMG // 2
    factor = jnp.where(high_row, 2 * first[:, 0:1] + (P_SIZE - 1), 2 * first[:, 1:2])
    sign = jnp.where(high_row, -1.0, 1.0)

    def swap(x):
        return jnp.concatenate([x[:, four:], x[:, :four]], axis=1)

    def tabulate(lo, hi):
        count = hi - lo
        cells = buf[lo:hi, 1]
        half = cos_sin(cells * (math.pi / IMG))
        turns = cells.astype(jnp.int32) * factor[None]
        turns = turns + swap(turns)
        turns = ((turns + IMG) & (2 * IMG - 1)) - IMG
        base = square(cos_sin(turns.astype(jnp.float32) * (math.pi / (2 * IMG))))
        x = buf[lo:hi, 0] * jnp.stack(
            [jnp.broadcast_to(gains[j], (tall, LANES)) for j in range(lo, hi)]
        )
        amp[lo:hi] = x * base[0] + swap(x) * (base[1] * sign[None])
        half_c[lo:hi] = half[0]
        half_s[lo:hi] = half[1]
        z = square(half)
        one = (jnp.ones_like(z[0]), jnp.zeros_like(z[0]))
        fine = powers(z, FINE)
        fine[0] = one
        step_c[lo:hi], step_s[lo:hi] = square(fine[FINE // 2])
        for ref, part in ((fine_c, 0), (fine_s, 1)):
            for k, entry in enumerate(fine):
                for i in range(count):
                    at = ((lo + i) * FINE + k) * tall
                    ref[at:at + tall, :] = entry[part][i]

    def image_terms(slot, sums):
        cu, su, re, im = [], [], [], []
        for r in range(four):
            def pick(row):
                at = pl.ds(slot * (FINE * tall) + row, FINE, stride=tall)
                return fine_c[at, :], fine_s[at, :]

            def line(refs, row):
                return refs[0][slot, row:row + 1, :], refs[1][slot, row:row + 1, :]

            def climb(start, row, rows_at):
                step = line((step_c, step_s), row)
                double = jnp.broadcast_to(step[0] + step[0], (FINE, LANES))
                table = [start, times(step, start)]
                while len(table) * FINE < rows_at:
                    table.append(
                        tuple(double * now - past for past, now in zip(table[-2], table[-1]))
                    )
                return table

            u = times(line((half_c, half_s), r), pick(r))
            v = times(
                (amp[slot, r:r + 1, :], amp[slot, four + r:four + r + 1, :]),
                pick(four + r),
            )
            left = climb(u, r, HALF)
            right = climb(v, four + r, P_SIZE)
            for kept, table, part in ((cu, left, 0), (su, left, 1), (re, right, 0), (im, right, 1)):
                kept.append(
                    jnp.concatenate([entry[part] for entry in table], axis=0).astype(jnp.bfloat16)
                )
        cu, su, re, im = (jnp.concatenate(kept, axis=1) for kept in (cu, su, re, im))
        return (
            sums[0] + lax.dot_general(cu, re, NT, preferred_element_type=jnp.float32),
            sums[1] + lax.dot_general(su, im, NT, preferred_element_type=jnp.float32),
        )

    sums = (jnp.zeros((HALF, P_SIZE), jnp.float32),) * 2
    for lo, hi in arrival_groups(n):
        for j in range(max(lo, 1), hi):
            to_peer(j, peers[j], 0).wait_recv()
        tabulate(lo, hi)
        sums = lax.fori_loop(lo, hi, image_terms, sums, unroll=hi - lo if hi - lo <= 8 else 1)
    even, odd = sums

    share = P_SIZE // nf
    for f in range(nf):
        if f < nf // 2:
            at = (nf // 2 - 1 - f) * share
            stage[f] = even[at:at + share] + odd[at:at + share]
        else:
            at = (f - nf // 2) * share
            stage[f] = even[at:at + share] - odd[at:at + share]
    exchanges = []
    for j in reversed(range(1, nf)):
        to = partner(mf, j, nf)
        exchanges.append(
            pltpu.make_async_remote_copy(
                src_ref=stage.at[to],
                dst_ref=rbuf.at[j],
                send_sem=rsend_sem.at[j],
                recv_sem=rrecv_sem.at[j],
                device_id={"freq": to},
                device_id_type=MESH,
            )
        )
        exchanges[-1].start()
    total = stage[mf]
    for exchange in exchanges:
        exchange.wait_recv()
    for j in range(1, nf):
        total = total + rbuf[j]

    row8 = lax.broadcasted_iota(jnp.int32, (8, P_SIZE), 0)
    mirrored = []
    for k in reversed(range(share // 8)):
        y = pltpu.roll(total[k * 8:(k + 1) * 8], 4, 0)
        y = jnp.where((row8 & 2) != 0, pltpu.roll(y, 2, 0), pltpu.roll(y, 6, 0))
        y = jnp.where((row8 & 1) != 0, pltpu.roll(y, 1, 0), pltpu.roll(y, 7, 0))
        mirrored.append(y)
    mirrored = jnp.concatenate(mirrored, axis=0)
    out_ref[0] = jnp.where(mf < nf // 2, mirrored, total)
    for copy in sends + exchanges:
        copy.wait_send()


def body(n, nf, scale, visibilities, weights, uv_cells, flags, plan, beam, facets):
    blocks, _, rows = visibilities.shape
    four = blocks * (KEEP // LANES)
    tall = 2 * four
    share = P_SIZE // nf
    steps = plan.shape[0]
    f32, i32 = jnp.float32, jnp.int32
    return pl.pallas_call(
        functools.partial(kernel, n, nf, scale),
        out_shape=pltpu.VMEM((1, share, P_SIZE), f32),
        in_specs=[pl.BlockSpec(memory_space=pltpu.HBM)] * 7,
        out_specs=pl.BlockSpec(memory_space=pltpu.VMEM),
        scratch_shapes=[
            pltpu.VMEM((blocks, 2, rows), f32),
            pltpu.VMEM((blocks, rows), f32),
            pltpu.VMEM((blocks, 2, rows), i32),
            pltpu.VMEM((blocks, rows), i32),
            pltpu.VMEM((1, steps), i32),
            pltpu.VMEM((1, steps), f32),
            pltpu.VMEM((1, 2), i32),
            pltpu.VMEM((n, 2, tall, LANES), f32),
            pltpu.VMEM((n * FINE * tall, LANES), f32),
            pltpu.VMEM((n * FINE * tall, LANES), f32),
            pltpu.VMEM((n, tall, LANES), f32),
            pltpu.VMEM((n, tall, LANES), f32),
            pltpu.VMEM((n, tall, LANES), f32),
            pltpu.VMEM((n, tall, LANES), f32),
            pltpu.VMEM((n, tall, LANES), f32),
            pltpu.VMEM((nf, share, P_SIZE), f32),
            pltpu.VMEM((nf, share, P_SIZE), f32),
            pltpu.SemaphoreType.DMA((7,)),
            pltpu.SemaphoreType.DMA((n,)),
            pltpu.SemaphoreType.DMA((n,)),
            pltpu.SemaphoreType.DMA((nf,)),
            pltpu.SemaphoreType.DMA((nf,)),
        ],
        compiler_params=pltpu.CompilerParams(
            collective_id=0, has_side_effects=True, vmem_limit_bytes=62 * 1024 * 1024
        ),
        name="facet_image",
    )(visibilities, weights, uv_cells, flags, plan.reshape(1, steps), beam, facets)


def solution(mesh):
    n, nf = mesh.shape["facet"], mesh.shape["freq"]
    in_specs = (
        P("facet", None, "freq"),
        P("facet", "freq"),
        P("facet", None, "freq"),
        P("facet", "freq"),
        P(),
        P("facet", None),
        P("facet", None),
    )
    out_specs = P("facet", "freq", None)

    def whole(visibilities, *others):
        scale = 2.0 / math.sqrt(visibilities.shape[0] * visibilities.shape[2])
        return jax.shard_map(
            functools.partial(body, n, nf, scale),
            mesh=mesh, in_specs=in_specs, out_specs=out_specs, check_vma=False,
        )(visibilities, *others)

    return whole
```
